32 devices in a mesh: dp: 8 (over z, x), mp: 4 (over y, core).
Axes of the slice: x: 2, y: 2, z: 4, core: 2. Of those that a mesh axis runs over, the one named last changes fastest.
Arguments:
- partial_grads: bfloat16 [8, 1536, 2048], P('dp', None, 'mp'), may hold values from -1.75 to 1.75
- band_owner: int32 [8], replicated, may hold values from 0 to 7, as said below
- left_factor: float32 [1536, 2048], P('dp', 'mp'), may hold values from -1 to 2.5
- right_factor: float32 [1536, 2048], P('dp', 'mp'), may hold values from -1 to 2.5
- left_root: bfloat16 [1536, 2048], P('dp', 'mp'), may hold values from -1 to 2.5, as said below
- right_root: bfloat16 [1536, 2048], P('dp', 'mp'), may hold values from -1 to 2.5, as said below
Outputs:
- direction: bfloat16 [1536, 2048], P(None, 'mp')
- left_updated: float32 [1536, 2048], P('dp', 'mp')
- right_updated: float32 [1536, 2048], P('dp', 'mp')
The draws below stay inside these ranges and needn't reach their ends.
Inputs may be any that keep to these rules, and one draw needn't show every extreme that they name: `band_owner`: a permutation: every index of dp owns exactly one band. `left_root`: in band order, every 512 x 512 block is symmetric. `right_root`: in band order, every 512 x 512 block is symmetric.
All inputs are finite; a program needn't handle non-finite values.
Results may differ from the reference program's by a relative error of at most 0.01.
Values may be sent and summed in bfloat16 or wider, within the bound.
No kernel may reach another device: no remote copies, remote signals or barrier semaphores. Data moves between devices by JAX's collectives and lax.ppermute only.
A program may use at most 64 MiB of HBM per device.

```python
import jax
import jax.numpy as jnp
from jax import lax

BLK = 512
NB = 3
BAND = 192
N_DP = 8
N_MP = 4


def owner_table(key):
    return jax.random.permutation(jax.random.fold_in(key, 101), N_DP).astype(jnp.int32)


def symmetric_bands(key, salt_tag, floor_val, ceiling, spread):
    noise_key = jax.random.fold_in(key, salt_tag)
    diag_key = jax.random.fold_in(key, salt_tag + 1)
    howmany = NB * N_MP
    noise_vals = jnp.clip(jax.random.normal(noise_key, (howmany, BLK, BLK), jnp.float32), -4.0, 4.0)
    symmetric = (noise_vals + jnp.transpose(noise_vals, (0, 2, 1))) * (spread / jnp.sqrt(2.0 * BLK))
    diagonal = jnp.exp(jax.random.uniform(diag_key, (howmany, BLK), jnp.float32, jnp.log(floor_val), jnp.log(ceiling)))
    blocks = symmetric + diagonal[:, :, None] * jnp.eye(BLK, dtype=jnp.float32)[None]
    bands = blocks.reshape(NB, N_MP, BLK, BLK).transpose(0, 2, 1, 3).reshape(N_DP, BAND, N_MP * BLK)
    owners = owner_table(key)
    placed = jnp.zeros((N_DP, BAND, N_MP * BLK), jnp.float32).at[owners].set(bands)
    return placed.reshape(NB * BLK, N_MP * BLK)


def draw_band_owner(key, part):
    return owner_table(key)


def draw_left_factor(key, part):
    return symmetric_bands(key, 11, 0.5, 2.0, 0.25)


def draw_right_factor(key, part):
    return symmetric_bands(key, 21, 0.5, 2.0, 0.25)


def draw_left_root(key, part):
    return symmetric_bands(key, 31, 0.6, 1.8, 0.25).astype(jnp.bfloat16)


def draw_right_root(key, part):
    return symmetric_bands(key, 41, 0.6, 1.8, 0.25).astype(jnp.bfloat16)


def with_spikes(array, rng, source, target, blocks, factor):
    def block_of(position):
        return (jnp.arange(array.shape[position]) // (array.shape[position] // blocks)).reshape((-1,) + (1,) * (array.ndim - 1 - position))

    near = jax.random.permutation(rng, blocks)[block_of(target)]
    other_side = (block_of(target) + blocks // 2) % blocks
    return jnp.where((block_of(source) == near) | (block_of(source) == other_side), factor * array, array)


def block_scale(own_key, dims, cuts, smallest, largest):
    def one(dim, parts):
        heights = jax.random.uniform(jax.random.fold_in(jax.random.fold_in(own_key, 6), dim), (parts,), jnp.float32, smallest / len(cuts), largest / len(cuts))
        return jnp.repeat(jnp.exp(heights), dims[dim] // parts).reshape((-1,) + (1,) * (len(dims) - dim - 1))

    loudness = one(*cuts[0])
    for cut in cuts[1:]:
        loudness = loudness * one(*cut)
    return loudness


def noise_with(rng, extent, deviation, limit, pieces, heavy, kind=jnp.bfloat16):
    array = deviation * jax.random.normal(rng, extent, jnp.float32)
    if pieces:
        array = array * block_scale(rng, extent, pieces, -0.22, 0.18)
    return jnp.clip(with_spikes(array, jax.random.fold_in(rng, 3), *heavy), -limit, limit).astype(kind)


def setup_inputs(seed: int = 0) -> dict:
    key_of = jax.random.split(jax.random.key(seed), 7)
    return {
        "partial_grads": noise_with(key_of[0], (N_DP, NB * BLK, BLK * N_MP), (0.25 * N_DP ** -0.5), 1.75, ((0, 8), (2, 4)), (0, 1, 8, 2.0)),
        "band_owner": draw_band_owner(jax.random.fold_in(key_of[6], 71), 0),
        "left_factor": draw_left_factor(jax.random.fold_in(key_of[6], 71), 0),
        "right_factor": draw_right_factor(jax.random.fold_in(key_of[6], 71), 0),
        "left_root": draw_left_root(jax.random.fold_in(key_of[6], 71), 0),
        "right_root": draw_right_root(jax.random.fold_in(key_of[6], 71), 0),
    }


BETA = 0.95


def to_blocks(matrix):
    return matrix.reshape(NB, BLK, N_MP, BLK).transpose(0, 2, 1, 3)


def from_blocks(blocks):
    return blocks.transpose(0, 2, 1, 3).reshape(NB * BLK, N_MP * BLK)


def reference(partial_grads, band_owner, left_factor, right_factor, left_root, right_root):
    highest = lax.Precision.HIGHEST
    owners = band_owner.astype(jnp.int32)
    inverse = jnp.argsort(owners).astype(jnp.int32)

    def to_bands(stored):
        return stored.reshape(N_DP, BAND, N_MP * BLK)[owners].reshape(NB * BLK, N_MP * BLK)

    def to_devices(stored):
        return stored.reshape(N_DP, BAND, N_MP * BLK)[inverse].reshape(NB * BLK, N_MP * BLK)

    gradient = jnp.sum(partial_grads, axis=0, dtype=jnp.float32)
    grad16 = gradient.astype(jnp.bfloat16)
    gblocks = to_blocks(grad16).astype(jnp.float32)
    left_term = jnp.einsum('bmik,bmjk->bmij', gblocks, gblocks, precision=highest)
    right_term = jnp.einsum('bmki,bmkj->bmij', gblocks, gblocks, precision=highest)
    left_next = BETA * to_blocks(to_bands(left_factor)) + (1.0 - BETA) * left_term
    right_next = BETA * to_blocks(to_bands(right_factor)) + (1.0 - BETA) * right_term
    left_pre = to_blocks(to_bands(left_root)).astype(jnp.float32)
    right_pre = to_blocks(to_bands(right_root)).astype(jnp.float32)
    mixed = jnp.einsum('bmik,bmkj->bmij', gblocks, right_pre, precision=highest).astype(jnp.bfloat16)
    direction = jnp.einsum('bmik,bmkj->bmij', left_pre, mixed.astype(jnp.float32), precision=highest).astype(jnp.bfloat16)
    left_updated = to_devices(from_blocks(left_next))
    right_updated = to_devices(from_blocks(right_next))
    return from_blocks(direction), left_updated, right_updated
```

```python
import functools

import jax
import jax.numpy as jnp
from jax import lax
from jax.experimental import pallas as pl
from jax.experimental.pallas import tpu as pltpu
from jax.sharding import PartitionSpec as P

BETA = 0.95
TILE = 64
CHUNK = 32
F32 = jnp.float32
BF16 = jnp.bfloat16
NT = (((1,), (1,)), ((), ()))
VMEM_LIMIT = 40 * 1024 * 1024


def against(band_rows, whole_rows, select):
    nblocks = select.shape[1]
    breadth = whole_rows.shape[1]
    blocks = whole_rows.reshape(nblocks, breadth, breadth)
    products = jnp.einsum("rk,bck->rbc", band_rows, blocks, preferred_element_type=jnp.float32)
    return jnp.sum(select[:, :, None] * products, axis=1)


def to_band_order(gathered, owners, members):
    shaped = gathered.reshape(members, -1, gathered.shape[1])
    return jnp.take(shaped, owners, axis=0).reshape(gathered.shape)


def general(partial_grads, band_owner, left_factor, right_factor, left_root, right_root):
    members = lax.axis_size("dp")
    band_size = left_factor.shape[0]
    breadth = left_factor.shape[1]
    stacked = partial_grads.shape[1]
    nblocks = stacked // breadth
    devices = jnp.arange(members, dtype=jnp.int32)
    inverse = jnp.sum(
        jnp.where(band_owner[None, :] == devices[:, None], devices[None, :], 0), axis=1
    )
    own_band = inverse[lax.axis_index("dp")]
    partial_value = partial_grads[0]
    even_rows = lax.psum_scatter(
        partial_value.astype(jnp.float32), "dp", scatter_dimension=0, tiled=True
    ).astype(jnp.bfloat16)
    grad_full = lax.all_gather(even_rows, "dp", axis=0, tiled=True)
    grad_rows = lax.dynamic_slice_in_dim(grad_full, own_band * band_size, band_size, 0)
    global_rows = own_band * band_size + jnp.arange(band_size, dtype=jnp.int32)
    block_ids = global_rows // breadth
    within = global_rows % breadth
    block_range = jnp.arange(nblocks, dtype=jnp.int32)
    select = (block_ids[:, None] == block_range[None, :]).astype(jnp.float32)
    left_term = against(grad_rows, grad_full, select)
    left_updated = BETA * left_factor + (1.0 - BETA) * left_term
    column_range = jnp.arange(breadth, dtype=jnp.int32)
    onehot = (
        (block_range[:, None, None] == block_ids[None, None, :])
        & (column_range[None, :, None] == within[None, None, :])
    ).astype(jnp.bfloat16)
    blocks = grad_full.reshape(nblocks, breadth, breadth)
    columns = jnp.einsum("bkc,bcr->kr", blocks, onehot, preferred_element_type=jnp.float32).astype(
        jnp.bfloat16
    )
    right_products = jnp.einsum("kr,bkc->rbc", columns, blocks, preferred_element_type=jnp.float32)
    right_term = jnp.sum(select[:, :, None] * right_products, axis=1)
    right_updated = BETA * right_factor + (1.0 - BETA) * right_term
    mixed_rows = against(right_root, grad_full, select).astype(jnp.bfloat16)
    mixed_full = to_band_order(
        lax.all_gather(mixed_rows, "dp", axis=0, tiled=True), band_owner, members
    )
    direction_rows = against(left_root, mixed_full, select).astype(jnp.bfloat16)
    direction = to_band_order(
        lax.all_gather(direction_rows, "dp", axis=0, tiled=True), band_owner, members
    )
    return (direction, left_updated, right_updated)


def seat_of(device, n):
    return jnp.where((device & 1) == 0, device >> 1, n - ((device + 1) >> 1))


def device_at(seat, n):
    seat = jnp.where(seat < 0, seat + n, seat)
    seat = jnp.where(seat >= n, seat - n, seat)
    return jnp.where(seat < n // 2, 2 * seat, 2 * (n - 1 - seat) + 1)


def away(me, offset, n):
    return device_at(seat_of(me, n) + offset, n)


def band_of(owner_ref, device, n):
    band = jnp.int32(0)
    for k in range(n):
        band = band + jnp.where(owner_ref[k] == device, k, 0)
    return band


def whole(*shape):
    return pl.BlockSpec(shape, lambda i, *_: (0,) * len(shape))


def params(limit=VMEM_LIMIT):
    return pltpu.CompilerParams(vmem_limit_bytes=limit)


def first_sends(me, partial, n):
    band, breadth = partial.shape[1] // n, partial.shape[2]
    half = band // 2

    def kernel(me_ref, far_ref, right_ref, left_ref):
        right_ref[...] = far_ref[0, :half]
        left_ref[...] = far_ref[0, half:]

    out = jax.ShapeDtypeStruct((half, breadth), BF16)
    return pl.pallas_call(
        kernel,
        out_shape=(out, out),
        grid_spec=pltpu.PrefetchScalarGridSpec(
            num_scalar_prefetch=1,
            grid=(1,),
            in_specs=[
                pl.BlockSpec((1, band, breadth), lambda i, m: (0, away(m[0], n // 2, n), 0)),
            ],
            out_specs=(whole(half, breadth), whole(half, breadth)),
        ),
        compiler_params=params(),
        name="first_sends",
    )(me, partial)


def add_sends(me, partial, right, left, distance, n):
    band, breadth = partial.shape[1] // n, partial.shape[2]
    half = band // 2
    rows = right.shape[0]

    def kernel(me_ref, ahead_ref, behind_ref, r_ref, l_ref, right_ref, left_ref):
        if rows == half:
            right_ref[:half] = (ahead_ref[0, :half].astype(F32) + r_ref[...].astype(F32)).astype(BF16)
            right_ref[half:] = ahead_ref[0, half:]
            left_ref[half:] = (behind_ref[0, half:].astype(F32) + l_ref[...].astype(F32)).astype(BF16)
            left_ref[:half] = behind_ref[0, :half]
        else:
            right_ref[...] = (ahead_ref[0].astype(F32) + r_ref[...].astype(F32)).astype(BF16)
            left_ref[...] = (behind_ref[0].astype(F32) + l_ref[...].astype(F32)).astype(BF16)

    out = jax.ShapeDtypeStruct((band, breadth), BF16)
    return pl.pallas_call(
        kernel,
        out_shape=(out, out),
        grid_spec=pltpu.PrefetchScalarGridSpec(
            num_scalar_prefetch=1,
            grid=(1,),
            in_specs=[
                pl.BlockSpec((1, band, breadth), lambda i, m: (0, away(m[0], distance, n), 0)),
                pl.BlockSpec((1, band, breadth), lambda i, m: (0, away(m[0], -distance, n), 0)),
                whole(rows, breadth),
                whole(rows, breadth),
            ],
            out_specs=(whole(band, breadth), whole(band, breadth)),
        ),
        compiler_params=params(),
        name="add_sends",
    )(me, partial, partial, right, left)


def add_own(me, partial, right, left, n):
    band, breadth = partial.shape[1] // n, partial.shape[2]

    def kernel(me_ref, own_ref, r_ref, l_ref, out_ref):
        total = own_ref[0].astype(F32) + r_ref[...].astype(F32) + l_ref[...].astype(F32)
        out_ref[...] = total.astype(BF16)

    return pl.pallas_call(
        kernel,
        out_shape=jax.ShapeDtypeStruct((band, breadth), BF16),
        grid_spec=pltpu.PrefetchScalarGridSpec(
            num_scalar_prefetch=1,
            grid=(1,),
            in_specs=[
                pl.BlockSpec((1, band, breadth), lambda i, m: (0, m[0], 0)),
                whole(band, breadth),
                whole(band, breadth),
            ],
            out_specs=whole(band, breadth),
        ),
        compiler_params=params(),
        name="add_own",
    )(me, partial, right, left)


def kept(breadth):
    return breadth // 2 + TILE


def pack_roots(me, owner, left_root, right_root, n):
    band, breadth = left_root.shape
    tiles = breadth // TILE
    width = kept(breadth)
    edge = width - TILE

    def kernel(me_ref, owner_ref, l_ref, r_ref, out_ref):
        k = band_of(owner_ref, me_ref[0], n)
        low = lax.broadcasted_iota(jnp.int32, (TILE, 2 * TILE), 1) < TILE
        for row in range(0, band, TILE):
            tile = ((k * band + row) // TILE) % tiles
            rows = slice(row, row + TILE)
            left = pltpu.roll(l_ref[rows].astype(F32), ((tiles - tile) % tiles) * TILE, 1)
            right = pltpu.roll(r_ref[rows].astype(F32), ((tiles - tile + 1) % tiles) * TILE, 1)
            out_ref[rows, :edge] = left[:, :edge].astype(BF16)
            out_ref[rows, edge : edge + 2 * TILE] = jnp.where(
                low, left[:, edge : edge + 2 * TILE], right[:, : 2 * TILE]
            ).astype(BF16)
            out_ref[rows, edge + 2 * TILE :] = right[:, 2 * TILE : width + TILE].astype(BF16)

    return pl.pallas_call(
        kernel,
        out_shape=jax.ShapeDtypeStruct((band, 2 * width), BF16),
        grid_spec=pltpu.PrefetchScalarGridSpec(
            num_scalar_prefetch=2,
            grid=(1,),
            in_specs=[whole(band, breadth), whole(band, breadth)],
            out_specs=whole(band, 2 * width),
        ),
        compiler_params=params(),
        name="pack_roots",
    )(me, owner, left_root, right_root)


def unpack_roots(me, owner, pieces, stacked, breadth, n):
    band = stacked // n
    tiles = breadth // TILE
    width = kept(breadth)
    edge = width - TILE
    nblocks = stacked // breadth

    def kernel(me_ref, owner_ref, *refs):
        refs, (left_ref, right_ref, half_l, half_r) = refs[: len(pieces)], refs[len(pieces) :]
        span = edge + 2 * TILE
        lane = lax.broadcasted_iota(jnp.int32, (CHUNK, span), 1)
        rest = jnp.zeros((CHUNK, breadth - span), F32)
        bands = {}
        for (offset, first, _), ref in zip(pieces, refs):
            if offset not in bands:
                bands[offset] = band_of(owner_ref, away(me_ref[0], offset, n), n)
            for row in range(0, ref.shape[0], CHUNK):
                place = bands[offset] * band + first + row
                tile = (place // TILE) % tiles
                left = jnp.where(lane < width, ref[row : row + CHUNK, :span].astype(F32), 0.0)
                left = pltpu.roll(jnp.concatenate([left, rest], 1), tile * TILE, 1)
                right = jnp.where(lane >= TILE, ref[row : row + CHUNK, edge:].astype(F32), 0.0)
                right = pltpu.roll(
                    jnp.concatenate([right, rest], 1), ((tile + tiles - 1) % tiles) * TILE, 1
                )
                at = pl.ds(pl.multiple_of(place, CHUNK), CHUNK)
                half_l[at, :] = left.astype(BF16)
                half_r[at, :] = right.astype(BF16)
        down = lax.broadcasted_iota(jnp.int32, (breadth, breadth), 0)
        over = lax.broadcasted_iota(jnp.int32, (breadth, breadth), 1)
        apart = (over // TILE - down // TILE + tiles) % tiles
        mirrored = (apart > 0) & (apart < tiles // 2)
        eye = (down == over).astype(BF16)
        for half, out in ((half_l, left_ref), (half_r, right_ref)):
            for b in range(nblocks):
                rows = slice(b * breadth, (b + 1) * breadth)
                upper = half[rows]
                flipped = lax.dot_general(
                    eye,
                    jnp.where(mirrored, upper, jnp.zeros_like(upper)),
                    NT,
                    preferred_element_type=F32,
                )
                out[rows] = (upper.astype(F32) + flipped).astype(BF16)

    out = jax.ShapeDtypeStruct((stacked, breadth), BF16)
    return pl.pallas_call(
        kernel,
        out_shape=(out, out),
        grid_spec=pltpu.PrefetchScalarGridSpec(
            num_scalar_prefetch=2,
            grid=(1,),
            in_specs=[whole(*x.shape) for _, _, x in pieces],
            out_specs=(whole(stacked, breadth), whole(stacked, breadth)),
            scratch_shapes=[pltpu.VMEM((stacked, breadth), BF16)] * 2,
        ),
        compiler_params=params(),
        name="unpack_roots",
    )(me, owner, *[x for _, _, x in pieces])


def finish(me, owner, pieces, left_root, right_root, left_factor, right_factor, n):
    stacked, breadth = left_root.shape
    band = stacked // n
    nblocks = stacked // breadth

    def kernel(me_ref, owner_ref, *refs):
        parts, refs = refs[: len(pieces)], refs[len(pieces) :]
        lroot, rroot, lfac, rfac, dir_ref, lout, rout, grad = refs
        for (offset, first, _), ref in zip(pieces, parts):
            place = away(me_ref[0], offset, n) * band + first
            grad[pl.ds(pl.multiple_of(place, CHUNK), ref.shape[0]), :] = ref[...]
        for b in range(nblocks):
            rows = slice(b * breadth, (b + 1) * breadth)
            mixed = jnp.dot(grad[rows], rroot[rows], preferred_element_type=F32).astype(BF16)
            dir_ref[rows] = jnp.dot(lroot[rows], mixed, preferred_element_type=F32).astype(BF16)
        start = band_of(owner_ref, me_ref[0], n) * band
        mine = grad[pl.ds(pl.multiple_of(start, CHUNK), band), :]
        first_block = start // breadth
        last_block = (start + band - 1) // breadth
        row = start + lax.broadcasted_iota(jnp.int32, (band, breadth), 0)
        column = lax.broadcasted_iota(jnp.int32, (band, breadth), 1)

        def terms(block):
            g = grad[pl.ds(pl.multiple_of(block * breadth, breadth), breadth), :]
            left = lax.dot_general(mine, g, NT, preferred_element_type=F32)
            pick = (row - block * breadth == column).astype(BF16)
            turned = lax.dot_general(pick, g, NT, preferred_element_type=F32).astype(BF16)
            return left, jnp.dot(turned, g, preferred_element_type=F32)

        left, right = terms(first_block)
        lout[...] = BETA * lfac[...] + (1.0 - BETA) * left
        rout[...] = BETA * rfac[...] + (1.0 - BETA) * right

        @pl.when(last_block != first_block)
        def _():
            left, right = terms(last_block)
            later = row >= last_block * breadth
            lout[...] = jnp.where(later, BETA * lfac[...] + (1.0 - BETA) * left, lout[...])
            rout[...] = jnp.where(later, BETA * rfac[...] + (1.0 - BETA) * right, rout[...])

    own = jax.ShapeDtypeStruct((band, breadth), F32)
    return pl.pallas_call(
        kernel,
        out_shape=(jax.ShapeDtypeStruct((stacked, breadth), BF16), own, own),
        grid_spec=pltpu.PrefetchScalarGridSpec(
            num_scalar_prefetch=2,
            grid=(1,),
            in_specs=[whole(*x.shape) for _, _, x in pieces]
            + [whole(stacked, breadth)] * 2
            + [whole(band, breadth)] * 2,
            out_specs=(whole(stacked, breadth), whole(band, breadth), whole(band, breadth)),
            scratch_shapes=[pltpu.VMEM((stacked, breadth), BF16)],
        ),
        compiler_params=params(),
        name="finish",
    )(me, owner, *[x for _, _, x in pieces], left_root, right_root, left_factor, right_factor)


def ring(n, partial_grads, band_owner, left_factor, right_factor, left_root, right_root):
    stacked, breadth = partial_grads.shape[1:]
    band = stacked // n
    half = band // 2
    me = lax.axis_index("dp").astype(jnp.int32).reshape(1)
    order = [2 * q for q in range(n // 2)] + [2 * (n - 1 - q) + 1 for q in range(n // 2, n)]
    onward = [(order[q], order[(q + 1) % n]) for q in range(n)]
    backward = [(b, a) for a, b in onward]

    def send_right(x):
        return lax.ppermute(x, "dp", onward)

    def send_left(x):
        return lax.ppermute(x, "dp", backward)

    def gather(own):
        pieces = [(0, 0, own)]
        right, left = own, own
        for hop in range(1, n // 2):
            right, left = send_right(right), send_left(left)
            pieces += [(-hop, 0, right), (hop, 0, left)]
        cut = own.shape[0] // 2
        pieces.append((n // 2, 0, send_right(right[:cut])))
        pieces.append((n // 2, cut, send_left(left[cut:])))
        return pieces

    right, left = first_sends(me, partial_grads, n)
    right, left = send_right(right), send_left(left)
    for distance in range(n // 2 - 1, 0, -1):
        right, left = add_sends(me, partial_grads, right, left, distance, n)
        right, left = send_right(right), send_left(left)
    own = add_own(me, partial_grads, right, left, n)
    packed = pack_roots(me, band_owner, left_root, right_root, n)
    roots = unpack_roots(me, band_owner, gather(packed), stacked, breadth, n)
    return finish(me, band_owner, gather(own), *roots, left_factor, right_factor, n)


def shards(n, partial_grads, *rest):
    stacked, breadth = partial_grads.shape[1:]
    band = stacked // n
    if 4 <= n <= 16 and n % 2 == 0 and band % TILE == 0 and breadth % (4 * TILE) == 0:
        return ring(n, partial_grads, *rest)
    return general(partial_grads, *rest)


def solution(mesh):
    placed = (P("dp", None, "mp"), P(), P("dp", "mp"), P("dp", "mp"), P("dp", "mp"), P("dp", "mp"))
    return jax.shard_map(
        functools.partial(shards, mesh.shape["dp"]),
        mesh=mesh,
        in_specs=placed,
        out_specs=(P(None, "mp"), P("dp", "mp"), P("dp", "mp")),
        check_vma=False,
    )
```

```python
import functools

import jax
import jax.numpy as jnp
from jax import lax
from jax.experimental import pallas as pl
from jax.experimental.pallas import tpu as pltpu
from jax.sharding import PartitionSpec as P

BETA = 0.95
TILE = 64
CHUNK = 32
GRAD_PARTS = 2
F32 = jnp.float32
BF16 = jnp.bfloat16
NT = (((1,), (1,)), ((), ()))
TN = (((0,), (0,)), ((), ()))
VMEM_LIMIT = 40 * 1024 * 1024
OPEN_LIMIT = 62 * 1024 * 1024


def against(band_rows, whole_rows, select):
    nblocks = select.shape[1]
    breadth = whole_rows.shape[1]
    blocks = whole_rows.reshape(nblocks, breadth, breadth)
    products = jnp.einsum("rk,bck->rbc", band_rows, blocks, preferred_element_type=jnp.float32)
    return jnp.sum(select[:, :, None] * products, axis=1)


def to_band_order(gathered, owners, members):
    shaped = gathered.reshape(members, -1, gathered.shape[1])
    return jnp.take(shaped, owners, axis=0).reshape(gathered.shape)


def general(partial_grads, band_owner, left_factor, right_factor, left_root, right_root):
    members = lax.axis_size("dp")
    band_size = left_factor.shape[0]
    breadth = left_factor.shape[1]
    stacked = partial_grads.shape[1]
    nblocks = stacked // breadth
    devices = jnp.arange(members, dtype=jnp.int32)
    inverse = jnp.sum(
        jnp.where(band_owner[None, :] == devices[:, None], devices[None, :], 0), axis=1
    )
    own_band = inverse[lax.axis_index("dp")]
    partial_value = partial_grads[0]
    even_rows = lax.psum_scatter(
        partial_value.astype(jnp.float32), "dp", scatter_dimension=0, tiled=True
    ).astype(jnp.bfloat16)
    grad_full = lax.all_gather(even_rows, "dp", axis=0, tiled=True)
    grad_rows = lax.dynamic_slice_in_dim(grad_full, own_band * band_size, band_size, 0)
    global_rows = own_band * band_size + jnp.arange(band_size, dtype=jnp.int32)
    block_ids = global_rows // breadth
    within = global_rows % breadth
    block_range = jnp.arange(nblocks, dtype=jnp.int32)
    select = (block_ids[:, None] == block_range[None, :]).astype(jnp.float32)
    left_term = against(grad_rows, grad_full, select)
    left_updated = BETA * left_factor + (1.0 - BETA) * left_term
    column_range = jnp.arange(breadth, dtype=jnp.int32)
    onehot = (
        (block_range[:, None, None] == block_ids[None, None, :])
        & (column_range[None, :, None] == within[None, None, :])
    ).astype(jnp.bfloat16)
    blocks = grad_full.reshape(nblocks, breadth, breadth)
    columns = jnp.einsum("bkc,bcr->kr", blocks, onehot, preferred_element_type=jnp.float32).astype(
        jnp.bfloat16
    )
    right_products = jnp.einsum("kr,bkc->rbc", columns, blocks, preferred_element_type=jnp.float32)
    right_term = jnp.sum(select[:, :, None] * right_products, axis=1)
    right_updated = BETA * right_factor + (1.0 - BETA) * right_term
    mixed_rows = against(right_root, grad_full, select).astype(jnp.bfloat16)
    mixed_full = to_band_order(
        lax.all_gather(mixed_rows, "dp", axis=0, tiled=True), band_owner, members
    )
    direction_rows = against(left_root, mixed_full, select).astype(jnp.bfloat16)
    direction = to_band_order(
        lax.all_gather(direction_rows, "dp", axis=0, tiled=True), band_owner, members
    )
    return (direction, left_updated, right_updated)


def seat_of(device, n):
    return jnp.where((device & 1) == 0, device >> 1, n - ((device + 1) >> 1))


def device_at(seat, n):
    seat = jnp.where(seat < 0, seat + n, seat)
    seat = jnp.where(seat >= n, seat - n, seat)
    return jnp.where(seat < n // 2, 2 * seat, 2 * (n - 1 - seat) + 1)


def away(me, offset, n):
    return device_at(seat_of(me, n) + offset, n)


def band_of(owner_ref, device, n):
    band = jnp.int32(0)
    for k in range(n):
        band = band + jnp.where(owner_ref[k] == device, k, 0)
    return band


def whole(*shape):
    return pl.BlockSpec(shape, lambda i, *_: (0,) * len(shape))


def params(limit=VMEM_LIMIT):
    return pltpu.CompilerParams(vmem_limit_bytes=limit)


def add_send(me, partial, arrived, distance, n, first, *after):
    band, breadth = partial.shape[1] // n, partial.shape[2]
    rows = arrived.shape[0]

    def kernel(me_ref, own_ref, a_ref, *refs):
        out_ref = refs[-1]
        if rows == band:
            out_ref[...] = (own_ref[0].astype(F32) + a_ref[...].astype(F32)).astype(BF16)
        else:
            got, other = slice(first, first + rows), slice(rows - first, band - first)
            out_ref[got] = (own_ref[0, got].astype(F32) + a_ref[...].astype(F32)).astype(BF16)
            out_ref[other] = own_ref[0, other]

    return pl.pallas_call(
        kernel,
        out_shape=jax.ShapeDtypeStruct((band, breadth), BF16),
        grid_spec=pltpu.PrefetchScalarGridSpec(
            num_scalar_prefetch=1,
            grid=(1,),
            in_specs=[
                pl.BlockSpec((1, band, breadth), lambda i, m: (0, away(m[0], distance, n), 0)),
                whole(rows, breadth),
            ]
            + [pl.BlockSpec(memory_space=pl.ANY)] * len(after),
            out_specs=whole(band, breadth),
        ),
        compiler_params=params(),
        name="add_send",
    )(me, partial, arrived, *after)


def add_own(me, partial, right, left, n, *after):
    band, breadth = partial.shape[1] // n, partial.shape[2]

    def kernel(me_ref, own_ref, r_ref, l_ref, *refs):
        out_ref = refs[-1]
        total = own_ref[0].astype(F32) + r_ref[...].astype(F32) + l_ref[...].astype(F32)
        out_ref[...] = total.astype(BF16)

    return pl.pallas_call(
        kernel,
        out_shape=jax.ShapeDtypeStruct((band, breadth), BF16),
        grid_spec=pltpu.PrefetchScalarGridSpec(
            num_scalar_prefetch=1,
            grid=(1,),
            in_specs=[
                pl.BlockSpec((1, band, breadth), lambda i, m: (0, m[0], 0)),
                whole(band, breadth),
                whole(band, breadth),
            ]
            + [pl.BlockSpec(memory_space=pl.ANY)] * len(after),
            out_specs=whole(band, breadth),
        ),
        compiler_params=params(),
        name="add_own",
    )(me, partial, right, left, *after)


PAIR = 2 * TILE


def kept(breadth):
    return breadth // 2 + TILE


def pairs_of(tile, breadth):
    pairs = breadth // PAIR
    odd = tile & 1
    whole_pair = (tile + odd) >> 1
    half_pair = whole_pair + pairs // 2 + (pairs // 2 - 1) * odd
    return whole_pair, half_pair, odd == 0


def lanes(pair, breadth):
    return pl.ds(pl.multiple_of((pair & (breadth // PAIR - 1)) * PAIR, PAIR), PAIR)


def open_ring(me, owner, partial, left_root, right_root, n):
    band, breadth = left_root.shape
    half = band // 2
    tiles = breadth // TILE
    whole_pairs = tiles // 4
    width = kept(breadth)

    def kernel(me_ref, owner_ref, p_ref, lr_ref, rr_ref, right_ref, left_ref, out_ref, l_ref, r_ref, sems):
        start = away(me_ref[0], n // 2, n) * band
        copies = [
            pltpu.make_async_copy(lr_ref, l_ref, sems.at[0]),
            pltpu.make_async_copy(rr_ref, r_ref, sems.at[1]),
            pltpu.make_async_copy(
                p_ref.at[0, pl.ds(pl.multiple_of(start, half), half)], right_ref, sems.at[2]
            ),
            pltpu.make_async_copy(
                p_ref.at[0, pl.ds(pl.multiple_of(start + half, half), half)], left_ref, sems.at[3]
            ),
        ]
        for copy in copies:
            copy.start()
        k = band_of(owner_ref, me_ref[0], n)
        low = lax.broadcasted_iota(jnp.int32, (TILE, PAIR), 1) < TILE
        copies[0].wait()
        copies[1].wait()
        for row in range(0, band, TILE):
            tile = (k * (band // TILE) + row // TILE) & (tiles - 1)
            first, half_pair, even = pairs_of(tile, breadth)
            rows = slice(row, row + TILE)
            for i in range(whole_pairs):
                pair = lanes(first + i, breadth)
                out_ref[rows, i * PAIR : (i + 1) * PAIR] = l_ref[rows, pair]
                out_ref[rows, (whole_pairs + i) * PAIR : (whole_pairs + i + 1) * PAIR] = r_ref[rows, pair]
            left = l_ref[rows, lanes(half_pair, breadth)].astype(F32)
            right = pltpu.roll(r_ref[rows, lanes(half_pair, breadth)].astype(F32), TILE, 1)
            mine = jnp.where(low == even, left, right)
            out_ref[rows, 2 * whole_pairs * PAIR :] = mine.astype(BF16)
        copies[2].wait()
        copies[3].wait()

    sent = jax.ShapeDtypeStruct((half, breadth), BF16)
    return pl.pallas_call(
        kernel,
        out_shape=(sent, sent, jax.ShapeDtypeStruct((band, 2 * width), BF16)),
        grid_spec=pltpu.PrefetchScalarGridSpec(
            num_scalar_prefetch=2,
            grid=(1,),
            in_specs=[pl.BlockSpec(memory_space=pltpu.HBM)] * 3,
            out_specs=(whole(half, breadth), whole(half, breadth), whole(band, 2 * width)),
            scratch_shapes=[pltpu.VMEM((band, breadth), BF16)] * 2 + [pltpu.SemaphoreType.DMA((4,))],
        ),
        compiler_params=params(OPEN_LIMIT),
        name="open_ring",
    )(me, owner, partial, left_root, right_root)


def unpack_roots(me, owner, pieces, stacked, breadth, n):
    band = stacked // n
    tiles = breadth // TILE
    whole_pairs = tiles // 4
    nblocks = stacked // breadth

    def kernel(me_ref, owner_ref, *refs):
        refs, (left_ref, right_ref, half_l, half_r) = refs[: len(pieces)], refs[len(pieces) :]
        lower = lax.broadcasted_iota(jnp.int32, (TILE, PAIR), 1) < TILE
        nothing = jnp.zeros((TILE, PAIR), BF16)
        bands = {}
        for (offset, first, _), ref in zip(pieces, refs):
            if offset not in bands:
                bands[offset] = band_of(owner_ref, away(me_ref[0], offset, n), n)
            edges = sorted({first, first + ref.shape[0], *range(0, band + 1, TILE)})
            edges = [x for x in edges if first <= x <= first + ref.shape[0]]
            for row, end in zip(edges[:-1], edges[1:]):
                tile = (bands[offset] * (band // TILE) + row // TILE) & (tiles - 1)
                start, half_pair, even = pairs_of(tile, breadth)
                at = pl.ds(pl.multiple_of(bands[offset] * band + row, CHUNK), end - row)
                rows = slice(row - first, end - first)
                low = lower[: end - row]
                zeros = nothing[: end - row]
                shared = ref[rows, 2 * whole_pairs * PAIR :].astype(F32)
                left = jnp.where(low == even, shared, 0.0).astype(BF16)
                right = jnp.where(low == even, pltpu.roll(shared, TILE, 1), 0.0).astype(BF16)
                for i in range(2 * whole_pairs):
                    pair = lanes(start + i, breadth)
                    if i < whole_pairs:
                        half_l[at, pair] = ref[rows, i * PAIR : (i + 1) * PAIR]
                        half_r[at, pair] = ref[
                            rows, (whole_pairs + i) * PAIR : (whole_pairs + i + 1) * PAIR
                        ]
                    else:
                        half_l[at, pair] = zeros
                        half_r[at, pair] = zeros
                half_l[at, lanes(half_pair, breadth)] = left
                half_r[at, lanes(half_pair, breadth)] = right
        shift = TILE.bit_length() - 1
        down = lax.broadcasted_iota(jnp.int32, (breadth, breadth), 0) >> shift
        over = lax.broadcasted_iota(jnp.int32, (breadth, breadth), 1) >> shift
        apart = over - down + jnp.where(over < down, tiles, 0)
        mirrored = (apart > 0) & (apart < tiles // 2)
        for half, out in ((half_r, right_ref), (half_l, left_ref)):
            for b in range(nblocks):
                rows = slice(b * breadth, (b + 1) * breadth)
                upper = half[rows]
                out[rows] = upper + jnp.where(mirrored, upper, jnp.zeros_like(upper)).T

    out = jax.ShapeDtypeStruct((stacked, breadth), BF16)
    return pl.pallas_call(
        kernel,
        out_shape=(out, out),
        grid_spec=pltpu.PrefetchScalarGridSpec(
            num_scalar_prefetch=2,
            grid=(1,),
            in_specs=[whole(*x.shape) for _, _, x in pieces],
            out_specs=(whole(stacked, breadth), whole(stacked, breadth)),
            scratch_shapes=[pltpu.VMEM((stacked, breadth), BF16)] * 2,
        ),
        compiler_params=params(),
        name="unpack_roots",
    )(me, owner, *[x for _, _, x in pieces])


def begin(me, pieces, left_root, right_root, n):
    stacked, breadth = left_root.shape
    band = stacked // n
    nblocks = stacked // breadth

    def kernel(me_ref, *refs):
        parts, refs = refs[: len(pieces)], refs[len(pieces) :]
        lroot, rroot, dir_ref, grad, rest_ref = refs
        for (offset, first, _), ref in zip(pieces, parts):
            place = away(me_ref[0], offset, n) * band + first
            grad[pl.ds(pl.multiple_of(place, CHUNK), ref.shape[0]), :] = ref[...]
        start = away(me_ref[0], n // 2, n) * band
        grad[pl.ds(pl.multiple_of(start, CHUNK), band), :] = jnp.zeros((band, breadth), BF16)
        for b in range(nblocks):
            rows = slice(b * breadth, (b + 1) * breadth)
            mixed = jnp.dot(grad[rows], rroot[rows], preferred_element_type=F32).astype(BF16)
            block = jnp.dot(lroot[rows], mixed, preferred_element_type=F32)
            dir_ref[rows] = block.astype(BF16)
            for slot, at in enumerate((start, start + band - 1)):

                @pl.when(at >> (breadth.bit_length() - 1) == b)
                def _():
                    rest_ref[slot] = block

    return pl.pallas_call(
        kernel,
        out_shape=(
            jax.ShapeDtypeStruct((stacked, breadth), BF16),
            jax.ShapeDtypeStruct((stacked, breadth), BF16),
            jax.ShapeDtypeStruct((2, breadth, breadth), F32),
        ),
        grid_spec=pltpu.PrefetchScalarGridSpec(
            num_scalar_prefetch=1,
            grid=(1,),
            in_specs=[whole(*x.shape) for _, _, x in pieces] + [whole(stacked, breadth)] * 2,
            out_specs=(
                whole(stacked, breadth),
                whole(stacked, breadth),
                whole(2, breadth, breadth),
            ),
        ),
        compiler_params=params(),
        name="begin",
    )(me, *[x for _, _, x in pieces], left_root, right_root)


def finish(me, owner, pieces, directions, grad, rest, left_root, right_root, left_factor, right_factor, n):
    stacked, breadth = left_root.shape
    band = stacked // n

    def kernel(me_ref, owner_ref, *refs):
        parts, refs = refs[: len(pieces)], refs[len(pieces) :]
        _, grad_ref, rest_ref, lroot, rroot, lfac, rfac, *refs = refs
        dir_ref, lout_ref, rout_ref, late, block, lout, rout, sems = refs
        far = away(me_ref[0], n // 2, n) * band
        for (_, first, _), ref in zip(pieces, parts):
            late[first : first + ref.shape[0]] = ref[...]
        shift = breadth.bit_length() - 1
        row = (far + lax.broadcasted_iota(jnp.int32, (band, breadth), 0)) >> shift
        there = pl.ds(pl.multiple_of(far, CHUNK), band)
        first_block = far >> shift
        last_block = (far + band - 1) >> shift

        def span(number):
            return pl.ds(pl.multiple_of(number * breadth, breadth), breadth)

        def copy(slot, number):
            return pltpu.make_async_copy(block.at[slot], dir_ref.at[span(number)], sems.at[slot])

        def complete(slot, number):
            some = jnp.where(row == number, late[...].astype(F32), 0.0).astype(BF16)
            mixed = jnp.dot(some, rroot[span(number), :], preferred_element_type=F32).astype(BF16)
            more = lax.dot_general(lroot[there, :], mixed, TN, preferred_element_type=F32)
            block[slot] = (rest_ref[slot] + more).astype(BF16)
            copy(slot, number).start()

        complete(0, first_block)

        @pl.when(last_block != first_block)
        def _():
            complete(1, last_block)

        start = band_of(owner_ref, me_ref[0], n) * band
        grad_ref[there, :] = late[...]
        mine = grad_ref[pl.ds(pl.multiple_of(start, CHUNK), band), :]
        own_first = start >> shift
        own_last = (start + band - 1) >> shift
        own_row = start + lax.broadcasted_iota(jnp.int32, (band, breadth), 0)
        column = lax.broadcasted_iota(jnp.int32, (band, breadth), 1)

        def left_term(number):
            return lax.dot_general(mine, grad_ref[span(number), :], NT, preferred_element_type=F32)

        def right_term(number):
            g = grad_ref[span(number), :]
            pick = (own_row - number * breadth == column).astype(BF16)
            turned = lax.dot_general(pick, g, NT, preferred_element_type=F32).astype(BF16)
            return jnp.dot(turned, g, preferred_element_type=F32)

        later = own_row >= own_last * breadth
        outs = []
        for slot, (term, fac, out, ref) in enumerate(
            ((left_term, lfac, lout, lout_ref), (right_term, rfac, rout, rout_ref))
        ):
            out[...] = BETA * fac[...] + (1.0 - BETA) * term(own_first)

            @pl.when(own_last != own_first)
            def _():
                new = BETA * fac[...] + (1.0 - BETA) * term(own_last)
                out[...] = jnp.where(later, new, out[...])

            outs.append(pltpu.make_async_copy(out, ref, sems.at[2 + slot]))
            outs[-1].start()
        copy(0, first_block).wait()

        @pl.when(last_block != first_block)
        def _():
            copy(1, last_block).wait()

        for out in outs:
            out.wait()

    own = jax.ShapeDtypeStruct((band, breadth), F32)
    return pl.pallas_call(
        kernel,
        out_shape=(jax.ShapeDtypeStruct((stacked, breadth), BF16), own, own),
        grid_spec=pltpu.PrefetchScalarGridSpec(
            num_scalar_prefetch=2,
            grid=(1,),
            in_specs=[whole(*x.shape) for _, _, x in pieces]
            + [pl.BlockSpec(memory_space=pl.ANY), whole(stacked, breadth), whole(2, breadth, breadth)]
            + [whole(stacked, breadth)] * 2
            + [whole(band, breadth)] * 2,
            out_specs=[pl.BlockSpec(memory_space=pl.ANY)] * 3,
            scratch_shapes=[
                pltpu.VMEM((band, breadth), BF16),
                pltpu.VMEM((2, breadth, breadth), BF16),
                pltpu.VMEM((band, breadth), F32),
                pltpu.VMEM((band, breadth), F32),
                pltpu.SemaphoreType.DMA((4,)),
            ],
        ),
        input_output_aliases={2 + len(pieces): 0},
        compiler_params=params(),
        name="finish",
    )(
        me,
        owner,
        *[x for _, _, x in pieces],
        directions,
        grad,
        rest,
        left_root,
        right_root,
        left_factor,
        right_factor,
    )


def ring(n, partial_grads, band_owner, left_factor, right_factor, left_root, right_root):
    stacked, breadth = partial_grads.shape[1:]
    band = stacked // n
    half = band // 2
    me = lax.axis_index("dp").astype(jnp.int32).reshape(1)
    order = [2 * q for q in range(n // 2)] + [2 * (n - 1 - q) + 1 for q in range(n // 2, n)]
    onward = [(order[q], order[(q + 1) % n]) for q in range(n)]
    backward = [(b, a) for a, b in onward]

    def send_right(x):
        return lax.ppermute(x, "dp", onward)

    def send_left(x):
        return lax.ppermute(x, "dp", backward)

    def gather(own, parts):
        rows = own.shape[0] // 2
        pieces = [(0, 0, own)]
        if parts == 1:
            right, left = own, own
            for hop in range(1, n // 2):
                right, left = send_right(right), send_left(left)
                pieces += [(-hop, 0, right), (hop, 0, left)]
            right, left = send_right(right[:rows]), send_left(left[rows:])
        else:
            upper, lower = own[:rows], own[rows:]
            ways = [upper, upper, lower, lower]
            for hop in range(1, n // 2):
                ways = [
                    send_right(ways[0]),
                    send_left(ways[1]),
                    send_right(ways[2]),
                    send_left(ways[3]),
                ]
                pieces += [(-hop, 0, ways[0]), (hop, 0, ways[1])]
                pieces += [(-hop, rows, ways[2]), (hop, rows, ways[3])]
            right, left = send_right(ways[0]), send_left(ways[3])
        return pieces + [(n // 2, 0, right), (n // 2, rows, left)]

    right, left, packed = open_ring(me, band_owner, partial_grads, left_root, right_root, n)
    right, left = send_right(right), send_left(left)
    root_pieces = gather(packed, 1)
    for distance in range(n // 2 - 1, 0, -1):
        right = add_send(me, partial_grads, right, distance, n, 0)
        left = add_send(me, partial_grads, left, -distance, n, half if left.shape[0] == half else 0)
        right, left = send_right(right), send_left(left)
    roots = unpack_roots(me, band_owner, root_pieces, stacked, breadth, n)
    own = add_own(me, partial_grads, right, left, n)
    pieces = gather(own, GRAD_PARTS)
    begun = begin(me, pieces[:-2], *roots, n)
    return finish(me, band_owner, pieces[-2:], *begun, *roots, left_factor, right_factor, n)


def shards(n, partial_grads, *rest):
    stacked, breadth = partial_grads.shape[1:]
    band = stacked // n
    fits = band % TILE == 0 and breadth % (4 * TILE) == 0 and breadth & (breadth - 1) == 0
    if 4 <= n <= 16 and n % 2 == 0 and fits:
        return ring(n, partial_grads, *rest)
    return general(partial_grads, *rest)


def solution(mesh):
    placed = (P("dp", None, "mp"), P(), P("dp", "mp"), P("dp", "mp"), P("dp", "mp"), P("dp", "mp"))
    return jax.shard_map(
        functools.partial(shards, mesh.shape["dp"]),
        mesh=mesh,
        in_specs=placed,
        out_specs=(P(None, "mp"), P("dp", "mp"), P("dp", "mp")),
        check_vma=False,
    )
```

```python
import functools

import jax
import jax.numpy as jnp
from jax import lax
from jax.experimental import pallas as pl
from jax.experimental.pallas import tpu as pltpu
from jax.sharding import PartitionSpec as P

BETA = 0.95
TILE = 64
CHUNK = 32
GRAD_PARTS = 2
F32 = jnp.float32
BF16 = jnp.bfloat16
NT = (((1,), (1,)), ((), ()))
TN = (((0,), (0,)), ((), ()))
VMEM_LIMIT = 40 * 1024 * 1024


def against(band_rows, whole_rows, select):
    nblocks = select.shape[1]
    breadth = whole_rows.shape[1]
    blocks = whole_rows.reshape(nblocks, breadth, breadth)
    products = jnp.einsum("rk,bck->rbc", band_rows, blocks, preferred_element_type=jnp.float32)
    return jnp.sum(select[:, :, None] * products, axis=1)


def to_band_order(gathered, owners, members):
    shaped = gathered.reshape(members, -1, gathered.shape[1])
    return jnp.take(shaped, owners, axis=0).reshape(gathered.shape)


def general(partial_grads, band_owner, left_factor, right_factor, left_root, right_root):
    members = lax.axis_size("dp")
    band_size = left_factor.shape[0]
    breadth = left_factor.shape[1]
    stacked = partial_grads.shape[1]
    nblocks = stacked // breadth
    devices = jnp.arange(members, dtype=jnp.int32)
    inverse = jnp.sum(
        jnp.where(band_owner[None, :] == devices[:, None], devices[None, :], 0), axis=1
    )
    own_band = inverse[lax.axis_index("dp")]
    partial_value = partial_grads[0]
    even_rows = lax.psum_scatter(
        partial_value.astype(jnp.float32), "dp", scatter_dimension=0, tiled=True
    ).astype(jnp.bfloat16)
    grad_full = lax.all_gather(even_rows, "dp", axis=0, tiled=True)
    grad_rows = lax.dynamic_slice_in_dim(grad_full, own_band * band_size, band_size, 0)
    global_rows = own_band * band_size + jnp.arange(band_size, dtype=jnp.int32)
    block_ids = global_rows // breadth
    within = global_rows % breadth
    block_range = jnp.arange(nblocks, dtype=jnp.int32)
    select = (block_ids[:, None] == block_range[None, :]).astype(jnp.float32)
    left_term = against(grad_rows, grad_full, select)
    left_updated = BETA * left_factor + (1.0 - BETA) * left_term
    column_range = jnp.arange(breadth, dtype=jnp.int32)
    onehot = (
        (block_range[:, None, None] == block_ids[None, None, :])
        & (column_range[None, :, None] == within[None, None, :])
    ).astype(jnp.bfloat16)
    blocks = grad_full.reshape(nblocks, breadth, breadth)
    columns = jnp.einsum("bkc,bcr->kr", blocks, onehot, preferred_element_type=jnp.float32).astype(
        jnp.bfloat16
    )
    right_products = jnp.einsum("kr,bkc->rbc", columns, blocks, preferred_element_type=jnp.float32)
    right_term = jnp.sum(select[:, :, None] * right_products, axis=1)
    right_updated = BETA * right_factor + (1.0 - BETA) * right_term
    mixed_rows = against(right_root, grad_full, select).astype(jnp.bfloat16)
    mixed_full = to_band_order(
        lax.all_gather(mixed_rows, "dp", axis=0, tiled=True), band_owner, members
    )
    direction_rows = against(left_root, mixed_full, select).astype(jnp.bfloat16)
    direction = to_band_order(
        lax.all_gather(direction_rows, "dp", axis=0, tiled=True), band_owner, members
    )
    return (direction, left_updated, right_updated)


def seat_of(device, n):
    return jnp.where((device & 1) == 0, device >> 1, n - ((device + 1) >> 1))


def device_at(seat, n):
    seat = jnp.where(seat < 0, seat + n, seat)
    seat = jnp.where(seat >= n, seat - n, seat)
    return jnp.where(seat < n // 2, 2 * seat, 2 * (n - 1 - seat) + 1)


def away(me, offset, n):
    return device_at(seat_of(me, n) + offset, n)


def band_of(owner_ref, device, n):
    band = jnp.int32(0)
    for k in range(n):
        band = band + jnp.where(owner_ref[k] == device, k, 0)
    return band


def whole(*shape):
    return pl.BlockSpec(shape, lambda i, *_: (0,) * len(shape))


def params(limit=VMEM_LIMIT):
    return pltpu.CompilerParams(vmem_limit_bytes=limit)


PAIR = 2 * TILE


def kept(breadth):
    return breadth // 2 + TILE


def pairs_of(tile, breadth):
    pairs = breadth // PAIR
    odd = tile & 1
    whole_pair = (tile + odd) >> 1
    half_pair = whole_pair + pairs // 2 + (pairs // 2 - 1) * odd
    return whole_pair, half_pair, odd == 0


def lanes(pair, breadth):
    return pl.ds(pl.multiple_of((pair & (breadth // PAIR - 1)) * PAIR, PAIR), PAIR)


def first_sends(me, partial, n):
    breadth = partial.shape[2]
    band = partial.shape[1] // n
    half = band // 2

    def kernel(me_ref, far_ref, right_ref, left_ref):
        right_ref[...] = far_ref[0, :half]
        left_ref[...] = far_ref[0, half:]

    sent = jax.ShapeDtypeStruct((half, breadth), BF16)
    return pl.pallas_call(
        kernel,
        out_shape=(sent, sent),
        grid_spec=pltpu.PrefetchScalarGridSpec(
            num_scalar_prefetch=1,
            grid=(1,),
            in_specs=[
                pl.BlockSpec((1, band, breadth), lambda i, m: (0, away(m[0], n // 2, n), 0)),
            ],
            out_specs=(whole(half, breadth), whole(half, breadth)),
        ),
        compiler_params=params(),
        name="first_sends",
    )(me, partial)


def pack_roots(me, owner, left_root, right_root, n):
    band, breadth = left_root.shape
    tiles = breadth // TILE
    whole_pairs = tiles // 4
    width = kept(breadth)

    def kernel(me_ref, owner_ref, l_ref, r_ref, out_ref):
        number = band_of(owner_ref, me_ref[0], n)
        low = lax.broadcasted_iota(jnp.int32, (TILE, PAIR), 1) < TILE
        for row in range(0, band, TILE):
            tile = (number * (band // TILE) + row // TILE) & (tiles - 1)
            first, half_pair, even = pairs_of(tile, breadth)
            rows = slice(row, row + TILE)
            for i in range(whole_pairs):
                pair = lanes(first + i, breadth)
                out_ref[rows, i * PAIR : (i + 1) * PAIR] = l_ref[rows, pair]
                out_ref[rows, (whole_pairs + i) * PAIR : (whole_pairs + i + 1) * PAIR] = r_ref[rows, pair]
            left = l_ref[rows, lanes(half_pair, breadth)].astype(F32)
            right = pltpu.roll(r_ref[rows, lanes(half_pair, breadth)].astype(F32), TILE, 1)
            mine = jnp.where(low == even, left, right)
            out_ref[rows, 2 * whole_pairs * PAIR :] = mine.astype(BF16)

    return pl.pallas_call(
        kernel,
        out_shape=jax.ShapeDtypeStruct((band, 2 * width), BF16),
        grid_spec=pltpu.PrefetchScalarGridSpec(
            num_scalar_prefetch=2,
            grid=(1,),
            in_specs=[whole(band, breadth), whole(band, breadth)],
            out_specs=whole(band, 2 * width),
        ),
        compiler_params=params(),
        name="pack_roots",
    )(me, owner, left_root, right_root)


def add_send(me, partial, arrived, distance, n, first, *after):
    band, breadth = partial.shape[1] // n, partial.shape[2]
    rows = arrived.shape[0]

    def kernel(me_ref, own_ref, a_ref, *refs):
        out_ref = refs[-1]
        if rows == band:
            out_ref[...] = (own_ref[0].astype(F32) + a_ref[...].astype(F32)).astype(BF16)
        else:
            got, other = slice(first, first + rows), slice(rows - first, band - first)
            out_ref[got] = (own_ref[0, got].astype(F32) + a_ref[...].astype(F32)).astype(BF16)
            out_ref[other] = own_ref[0, other]

    return pl.pallas_call(
        kernel,
        out_shape=jax.ShapeDtypeStruct((band, breadth), BF16),
        grid_spec=pltpu.PrefetchScalarGridSpec(
            num_scalar_prefetch=1,
            grid=(1,),
            in_specs=[
                pl.BlockSpec((1, band, breadth), lambda i, m: (0, away(m[0], distance, n), 0)),
                whole(rows, breadth),
            ]
            + [pl.BlockSpec(memory_space=pl.ANY)] * len(after),
            out_specs=whole(band, breadth),
        ),
        compiler_params=params(),
        name="add_send",
    )(me, partial, arrived, *after)


def add_own(me, partial, right, left, n, *after):
    band, breadth = partial.shape[1] // n, partial.shape[2]

    def kernel(me_ref, own_ref, r_ref, l_ref, *refs):
        out_ref = refs[-1]
        total = own_ref[0].astype(F32) + r_ref[...].astype(F32) + l_ref[...].astype(F32)
        out_ref[...] = total.astype(BF16)

    return pl.pallas_call(
        kernel,
        out_shape=jax.ShapeDtypeStruct((band, breadth), BF16),
        grid_spec=pltpu.PrefetchScalarGridSpec(
            num_scalar_prefetch=1,
            grid=(1,),
            in_specs=[
                pl.BlockSpec((1, band, breadth), lambda i, m: (0, m[0], 0)),
                whole(band, breadth),
                whole(band, breadth),
            ]
            + [pl.BlockSpec(memory_space=pl.ANY)] * len(after),
            out_specs=whole(band, breadth),
        ),
        compiler_params=params(),
        name="add_own",
    )(me, partial, right, left, *after)


def unpack_roots(me, owner, pieces, stacked, breadth, n):
    band = stacked // n
    tiles = breadth // TILE
    whole_pairs = tiles // 4
    nblocks = stacked // breadth

    def kernel(me_ref, owner_ref, *refs):
        refs, (left_ref, right_ref, half_l, half_r, table, sem) = refs[: len(pieces)], refs[len(pieces) :]
        copy = pltpu.make_async_copy(owner_ref, table, sem)
        copy.start()
        lower = lax.broadcasted_iota(jnp.int32, (TILE, PAIR), 1) < TILE
        nothing = jnp.zeros((TILE, PAIR), BF16)
        shift = TILE.bit_length() - 1
        down = lax.broadcasted_iota(jnp.int32, (breadth, breadth), 0) >> shift
        over = lax.broadcasted_iota(jnp.int32, (breadth, breadth), 1) >> shift
        apart = over - down + jnp.where(over < down, tiles, 0)
        mirrored = (apart > 0) & (apart < tiles // 2)
        copy.wait()
        numbers = {o: band_of(table, away(me_ref[0], o, n), n) for o in {p[0] for p in pieces}}
        for (offset, first, _), ref in zip(pieces, refs):
            number = numbers[offset]
            edges = sorted({first, first + ref.shape[0], *range(0, band + 1, TILE)})
            edges = [x for x in edges if first <= x <= first + ref.shape[0]]
            for row, end in zip(edges[:-1], edges[1:]):
                tile = (number * (band // TILE) + row // TILE) & (tiles - 1)
                start, half_pair, even = pairs_of(tile, breadth)
                at = pl.ds(pl.multiple_of(number * band + row, CHUNK), end - row)
                rows = slice(row - first, end - first)
                low = lower[: end - row]
                zeros = nothing[: end - row]
                shared = ref[rows, 2 * whole_pairs * PAIR :].astype(F32)
                left = jnp.where(low == even, shared, 0.0).astype(BF16)
                right = jnp.where(low == even, pltpu.roll(shared, TILE, 1), 0.0).astype(BF16)
                for i in range(2 * whole_pairs):
                    pair = lanes(start + i, breadth)
                    if i < whole_pairs:
                        half_l[at, pair] = ref[rows, i * PAIR : (i + 1) * PAIR]
                        half_r[at, pair] = ref[
                            rows, (whole_pairs + i) * PAIR : (whole_pairs + i + 1) * PAIR
                        ]
                    else:
                        half_l[at, pair] = zeros
                        half_r[at, pair] = zeros
                half_l[at, lanes(half_pair, breadth)] = left
                half_r[at, lanes(half_pair, breadth)] = right
        for half, out in ((half_r, right_ref), (half_l, left_ref)):
            for b in range(nblocks):
                rows = slice(b * breadth, (b + 1) * breadth)
                upper = half[rows]
                out[rows] = upper + jnp.where(mirrored, upper, jnp.zeros_like(upper)).T

    out = jax.ShapeDtypeStruct((stacked, breadth), BF16)
    return pl.pallas_call(
        kernel,
        out_shape=(out, out),
        grid_spec=pltpu.PrefetchScalarGridSpec(
            num_scalar_prefetch=1,
            grid=(1,),
            in_specs=[pl.BlockSpec(memory_space=pl.ANY)] + [whole(*x.shape) for _, _, x in pieces],
            out_specs=(whole(stacked, breadth), whole(stacked, breadth)),
            scratch_shapes=[pltpu.VMEM((stacked, breadth), BF16)] * 2
            + [pltpu.SMEM((n,), jnp.int32), pltpu.SemaphoreType.DMA],
        ),
        compiler_params=params(),
        name="unpack_roots",
    )(me, owner, *[x for _, _, x in pieces])


def begin(me, pieces, left_root, right_root, n):
    stacked, breadth = left_root.shape
    band = stacked // n
    nblocks = stacked // breadth

    def kernel(me_ref, *refs):
        parts, refs = refs[: len(pieces)], refs[len(pieces) :]
        lroot, rroot, dir_ref, grad, rest_ref = refs
        for (offset, first, _), ref in zip(pieces, parts):
            place = away(me_ref[0], offset, n) * band + first
            grad[pl.ds(pl.multiple_of(place, CHUNK), ref.shape[0]), :] = ref[...]
        start = away(me_ref[0], n // 2, n) * band
        grad[pl.ds(pl.multiple_of(start, CHUNK), band), :] = jnp.zeros((band, breadth), BF16)
        for b in range(nblocks):
            rows = slice(b * breadth, (b + 1) * breadth)
            mixed = jnp.dot(grad[rows], rroot[rows], preferred_element_type=F32).astype(BF16)
            block = jnp.dot(lroot[rows], mixed, preferred_element_type=F32)
            dir_ref[rows] = block.astype(BF16)
            for slot, at in enumerate((start, start + band - 1)):

                @pl.when(at >> (breadth.bit_length() - 1) == b)
                def _():
                    rest_ref[slot] = block

    return pl.pallas_call(
        kernel,
        out_shape=(
            jax.ShapeDtypeStruct((stacked, breadth), BF16),
            jax.ShapeDtypeStruct((stacked, breadth), BF16),
            jax.ShapeDtypeStruct((2, breadth, breadth), F32),
        ),
        grid_spec=pltpu.PrefetchScalarGridSpec(
            num_scalar_prefetch=1,
            grid=(1,),
            in_specs=[whole(*x.shape) for _, _, x in pieces] + [whole(stacked, breadth)] * 2,
            out_specs=(
                whole(stacked, breadth),
                whole(stacked, breadth),
                whole(2, breadth, breadth),
            ),
        ),
        compiler_params=params(),
        name="begin",
    )(me, *[x for _, _, x in pieces], left_root, right_root)


def finish(me, owner, pieces, directions, grad, rest, left_root, right_root, left_factor, right_factor, n):
    stacked, breadth = left_root.shape
    band = stacked // n
    nblocks = stacked // breadth

    def kernel(me_ref, owner_ref, *refs):
        parts, refs = refs[: len(pieces)], refs[len(pieces) :]
        part_ref, grad_ref, rest_ref, lroot, rroot, lfac, rfac, *refs = refs
        dir_ref, lout_ref, rout_ref, late, block, lout, rout, table, sems = refs
        lookup = pltpu.make_async_copy(owner_ref, table, sems.at[4 + nblocks])
        lookup.start()
        far = away(me_ref[0], n // 2, n) * band
        for (_, first, _), ref in zip(pieces, parts):
            late[first : first + ref.shape[0]] = ref[...]
        shift = breadth.bit_length() - 1
        row = (far + lax.broadcasted_iota(jnp.int32, (band, breadth), 0)) >> shift
        there = pl.ds(pl.multiple_of(far, CHUNK), band)
        first_block = far >> shift
        last_block = (far + band - 1) >> shift

        def span(number):
            return pl.ds(pl.multiple_of(number * breadth, breadth), breadth)

        def copy(slot, number):
            return pltpu.make_async_copy(block.at[slot], dir_ref.at[span(number)], sems.at[slot])

        def keep(b):
            rows = slice(b * breadth, (b + 1) * breadth)
            return pltpu.make_async_copy(part_ref.at[rows], dir_ref.at[rows], sems.at[4 + b])

        for b in range(nblocks):

            @pl.when((first_block != b) & (last_block != b))
            def _():
                keep(b).start()

        def complete(slot, number):
            some = jnp.where(row == number, late[...].astype(F32), 0.0).astype(BF16)
            mixed = jnp.dot(some, rroot[span(number), :], preferred_element_type=F32).astype(BF16)
            more = lax.dot_general(lroot[there, :], mixed, TN, preferred_element_type=F32)
            block[slot] = (rest_ref[slot] + more).astype(BF16)
            copy(slot, number).start()

        complete(0, first_block)

        @pl.when(last_block != first_block)
        def _():
            complete(1, last_block)

        lookup.wait()
        start = band_of(table, me_ref[0], n) * band
        grad_ref[there, :] = late[...]
        mine = grad_ref[pl.ds(pl.multiple_of(start, CHUNK), band), :]
        own_first = start >> shift
        own_last = (start + band - 1) >> shift
        own_row = start + lax.broadcasted_iota(jnp.int32, (band, breadth), 0)
        column = lax.broadcasted_iota(jnp.int32, (band, breadth), 1)

        def left_term(number):
            return lax.dot_general(mine, grad_ref[span(number), :], NT, preferred_element_type=F32)

        def right_term(number):
            g = grad_ref[span(number), :]
            pick = (own_row - number * breadth == column).astype(BF16)
            turned = lax.dot_general(pick, g, NT, preferred_element_type=F32).astype(BF16)
            return jnp.dot(turned, g, preferred_element_type=F32)

        later = own_row >= own_last * breadth
        outs = []
        for slot, (term, fac, out, ref) in enumerate(
            ((left_term, lfac, lout, lout_ref), (right_term, rfac, rout, rout_ref))
        ):
            out[...] = BETA * fac[...] + (1.0 - BETA) * term(own_first)

            @pl.when(own_last != own_first)
            def _():
                new = BETA * fac[...] + (1.0 - BETA) * term(own_last)
                out[...] = jnp.where(later, new, out[...])

            outs.append(pltpu.make_async_copy(out, ref, sems.at[2 + slot]))
            outs[-1].start()
        copy(0, first_block).wait()

        @pl.when(last_block != first_block)
        def _():
            copy(1, last_block).wait()

        for b in range(nblocks):

            @pl.when((first_block != b) & (last_block != b))
            def _():
                keep(b).wait()

        for out in outs:
            out.wait()

    own = jax.ShapeDtypeStruct((band, breadth), F32)
    return pl.pallas_call(
        kernel,
        out_shape=(jax.ShapeDtypeStruct((stacked, breadth), BF16), own, own),
        grid_spec=pltpu.PrefetchScalarGridSpec(
            num_scalar_prefetch=1,
            grid=(1,),
            in_specs=[pl.BlockSpec(memory_space=pl.ANY)]
            + [whole(*x.shape) for _, _, x in pieces]
            + [whole(stacked, breadth)] * 2
            + [whole(2, breadth, breadth)]
            + [whole(stacked, breadth)] * 2
            + [whole(band, breadth)] * 2,
            out_specs=[pl.BlockSpec(memory_space=pl.ANY)] * 3,
            scratch_shapes=[
                pltpu.VMEM((band, breadth), BF16),
                pltpu.VMEM((2, breadth, breadth), BF16),
                pltpu.VMEM((band, breadth), F32),
                pltpu.VMEM((band, breadth), F32),
                pltpu.SMEM((n,), jnp.int32),
                pltpu.SemaphoreType.DMA((5 + nblocks,)),
            ],
        ),
        compiler_params=params(),
        name="finish",
    )(
        me,
        owner,
        *[x for _, _, x in pieces],
        directions,
        grad,
        rest,
        left_root,
        right_root,
        left_factor,
        right_factor,
    )


def ring(n, partial_grads, band_owner, left_factor, right_factor, left_root, right_root):
    stacked, breadth = partial_grads.shape[1:]
    band = stacked // n
    half = band // 2
    me = lax.axis_index("dp").astype(jnp.int32).reshape(1)
    order = [2 * q for q in range(n // 2)] + [2 * (n - 1 - q) + 1 for q in range(n // 2, n)]
    onward = [(order[q], order[(q + 1) % n]) for q in range(n)]
    backward = [(b, a) for a, b in onward]

    def send_right(x):
        return lax.ppermute(x, "dp", onward)

    def send_left(x):
        return lax.ppermute(x, "dp", backward)

    def gather(own, parts):
        rows = own.shape[0] // 2
        pieces = [(0, 0, own)]
        if parts == 1:
            right, left = own, own
            for hop in range(1, n // 2):
                right, left = send_right(right), send_left(left)
                pieces += [(-hop, 0, right), (hop, 0, left)]
            right, left = send_right(right[:rows]), send_left(left[rows:])
        else:
            upper, lower = own[:rows], own[rows:]
            ways = [upper, upper, lower, lower]
            for hop in range(1, n // 2):
                ways = [
                    send_right(ways[0]),
                    send_left(ways[1]),
                    send_right(ways[2]),
                    send_left(ways[3]),
                ]
                pieces += [(-hop, 0, ways[0]), (hop, 0, ways[1])]
                pieces += [(-hop, rows, ways[2]), (hop, rows, ways[3])]
            right, left = send_right(ways[0]), send_left(ways[3])
        return pieces + [(n // 2, 0, right), (n // 2, rows, left)]

    right, left = first_sends(me, partial_grads, n)
    packed = pack_roots(me, band_owner, left_root, right_root, n)
    right, left = send_right(right), send_left(left)
    root_pieces = gather(packed, 1)
    for distance in range(n // 2 - 1, 0, -1):
        right = add_send(me, partial_grads, right, distance, n, 0)
        left = add_send(me, partial_grads, left, -distance, n, half if left.shape[0] == half else 0)
        right, left = send_right(right), send_left(left)
    roots = unpack_roots(me, band_owner, root_pieces, stacked, breadth, n)
    own = add_own(me, partial_grads, right, left, n)
    pieces = gather(own, GRAD_PARTS)
    begun = begin(me, pieces[:-2], *roots, n)
    return finish(me, band_owner, pieces[-2:], *begun, *roots, left_factor, right_factor, n)


def shards(n, partial_grads, *rest):
    stacked, breadth = partial_grads.shape[1:]
    band = stacked // n
    fits = band % TILE == 0 and breadth % (4 * TILE) == 0 and breadth & (breadth - 1) == 0
    if 4 <= n <= 16 and n % 2 == 0 and fits:
        return ring(n, partial_grads, *rest)
    return general(partial_grads, *rest)


def solution(mesh):
    placed = (P("dp", None, "mp"), P(), P("dp", "mp"), P("dp", "mp"), P("dp", "mp"), P("dp", "mp"))
    return jax.shard_map(
        functools.partial(shards, mesh.shape["dp"]),
        mesh=mesh,
        in_specs=placed,
        out_specs=(P(None, "mp"), P("dp", "mp"), P("dp", "mp")),
        check_vma=False,
    )
```

```python
import functools

import jax
import jax.numpy as jnp
from jax import lax
from jax.experimental import pallas as pl
from jax.experimental.pallas import tpu as pltpu
from jax.sharding import PartitionSpec as P

BETA = 0.95
TILE = 64
CHUNK = 32
GRAD_PARTS = 2
F32 = jnp.float32
BF16 = jnp.bfloat16
NT = (((1,), (1,)), ((), ()))
TN = (((0,), (0,)), ((), ()))
VMEM_LIMIT = 40 * 1024 * 1024


def against(band_rows, whole_rows, select):
    nblocks = select.shape[1]
    breadth = whole_rows.shape[1]
    blocks = whole_rows.reshape(nblocks, breadth, breadth)
    products = jnp.einsum("rk,bck->rbc", band_rows, blocks, preferred_element_type=jnp.float32)
    return jnp.sum(select[:, :, None] * products, axis=1)


def to_band_order(gathered, owners, members):
    shaped = gathered.reshape(members, -1, gathered.shape[1])
    return jnp.take(shaped, owners, axis=0).reshape(gathered.shape)


def general(partial_grads, band_owner, left_factor, right_factor, left_root, right_root):
    members = lax.axis_size("dp")
    band_size = left_factor.shape[0]
    breadth = left_factor.shape[1]
    stacked = partial_grads.shape[1]
    nblocks = stacked // breadth
    devices = jnp.arange(members, dtype=jnp.int32)
    inverse = jnp.sum(
        jnp.where(band_owner[None, :] == devices[:, None], devices[None, :], 0), axis=1
    )
    own_band = inverse[lax.axis_index("dp")]
    partial_value = partial_grads[0]
    even_rows = lax.psum_scatter(
        partial_value.astype(jnp.float32), "dp", scatter_dimension=0, tiled=True
    ).astype(jnp.bfloat16)
    grad_full = lax.all_gather(even_rows, "dp", axis=0, tiled=True)
    grad_rows = lax.dynamic_slice_in_dim(grad_full, own_band * band_size, band_size, 0)
    global_rows = own_band * band_size + jnp.arange(band_size, dtype=jnp.int32)
    block_ids = global_rows // breadth
    within = global_rows % breadth
    block_range = jnp.arange(nblocks, dtype=jnp.int32)
    select = (block_ids[:, None] == block_range[None, :]).astype(jnp.float32)
    left_term = against(grad_rows, grad_full, select)
    left_updated = BETA * left_factor + (1.0 - BETA) * left_term
    column_range = jnp.arange(breadth, dtype=jnp.int32)
    onehot = (
        (block_range[:, None, None] == block_ids[None, None, :])
        & (column_range[None, :, None] == within[None, None, :])
    ).astype(jnp.bfloat16)
    blocks = grad_full.reshape(nblocks, breadth, breadth)
    columns = jnp.einsum("bkc,bcr->kr", blocks, onehot, preferred_element_type=jnp.float32).astype(
        jnp.bfloat16
    )
    right_products = jnp.einsum("kr,bkc->rbc", columns, blocks, preferred_element_type=jnp.float32)
    right_term = jnp.sum(select[:, :, None] * right_products, axis=1)
    right_updated = BETA * right_factor + (1.0 - BETA) * right_term
    mixed_rows = against(right_root, grad_full, select).astype(jnp.bfloat16)
    mixed_full = to_band_order(
        lax.all_gather(mixed_rows, "dp", axis=0, tiled=True), band_owner, members
    )
    direction_rows = against(left_root, mixed_full, select).astype(jnp.bfloat16)
    direction = to_band_order(
        lax.all_gather(direction_rows, "dp", axis=0, tiled=True), band_owner, members
    )
    return (direction, left_updated, right_updated)


def seat_of(device, n):
    return jnp.where((device & 1) == 0, device >> 1, n - ((device + 1) >> 1))


def device_at(seat, n):
    seat = jnp.where(seat < 0, seat + n, seat)
    seat = jnp.where(seat >= n, seat - n, seat)
    return jnp.where(seat < n // 2, 2 * seat, 2 * (n - 1 - seat) + 1)


def away(me, offset, n):
    return device_at(seat_of(me, n) + offset, n)


def band_of(owner_ref, device, n):
    band = jnp.int32(0)
    for k in range(n):
        band = band + jnp.where(owner_ref[k] == device, k, 0)
    return band


def whole(*shape):
    return pl.BlockSpec(shape, lambda i, *_: (0,) * len(shape))


def params(limit=VMEM_LIMIT):
    return pltpu.CompilerParams(vmem_limit_bytes=limit)


PAIR = 2 * TILE


def meets(tile, tiles):
    half, quarter = tiles // 2, tiles // 4
    return ((tile < half) & (tile != quarter)) | (tile == half + quarter)


def slots_of(n, band, tiles):
    rows = band // TILE
    return max(sum(meets((k * rows + t) % tiles, tiles) for t in range(rows)) for k in range(n))


def lanes(pair, breadth):
    return pl.ds(pl.multiple_of((pair & (breadth // PAIR - 1)) * PAIR, PAIR), PAIR)


def lower_half(rows):
    return lax.broadcasted_iota(jnp.int32, (rows, PAIR), 1) < TILE


def swapped(x):
    return pltpu.roll(x, TILE, 1)


def first_sends(me, partial, n):
    breadth = partial.shape[2]
    band = partial.shape[1] // n
    half = band // 2

    def kernel(me_ref, far_ref, right_ref, left_ref):
        right_ref[...] = far_ref[0, :half]
        left_ref[...] = far_ref[0, half:]

    sent = jax.ShapeDtypeStruct((half, breadth), BF16)
    return pl.pallas_call(
        kernel,
        out_shape=(sent, sent),
        grid_spec=pltpu.PrefetchScalarGridSpec(
            num_scalar_prefetch=1,
            grid=(1,),
            in_specs=[
                pl.BlockSpec((1, band, breadth), lambda i, m: (0, away(m[0], n // 2, n), 0)),
            ],
            out_specs=(whole(half, breadth), whole(half, breadth)),
        ),
        compiler_params=params(),
        name="first_sends",
    )(me, partial)


def pack_roots(me, owner, left_root, right_root, n):
    band, breadth = left_root.shape
    tiles = breadth // TILE
    quarter = tiles // 4
    more = slots_of(n, band, tiles) * TILE * PAIR // breadth

    def kernel(me_ref, owner_ref, l_ref, r_ref, out_ref):
        number = band_of(owner_ref, me_ref[0], n)
        low = lower_half(TILE)
        out_ref[band:] = jnp.zeros((more, breadth), BF16)
        slot = jnp.int32(0)
        for row in range(0, band, TILE):
            tile = (number * (band // TILE) + row // TILE) & (tiles - 1)
            odd, pair = tile & 1, tile >> 1
            rows = slice(row, row + TILE)
            last = lanes(pair + quarter, breadth)
            for at, ref in ((0, l_ref), (quarter, r_ref)):
                start = ref[rows, lanes(pair, breadth)].astype(F32)
                end = ref[rows, last].astype(F32)
                mixed = jnp.where(low & (odd == 1), end, start).astype(BF16)
                out_ref[rows, at * PAIR : (at + 1) * PAIR] = mixed
                for i in range(1, quarter):
                    out_ref[rows, (at + i) * PAIR : (at + i + 1) * PAIR] = ref[rows, lanes(pair + i, breadth)]
            here = meets(tile, tiles)

            @pl.when(here)
            def _():
                left, right = l_ref[rows, last].astype(F32), r_ref[rows, last].astype(F32)
                left = jnp.where(odd == 1, swapped(left), left)
                right = jnp.where(odd == 1, right, swapped(right))
                both = jnp.where(low, left, right).astype(BF16)
                for i in range(TILE // more):
                    place = lanes(slot * (TILE // more) + i, breadth)
                    out_ref[band : band + more, place] = both[i * more : (i + 1) * more]

            slot = slot + here.astype(jnp.int32)

    return pl.pallas_call(
        kernel,
        out_shape=jax.ShapeDtypeStruct((band + more, breadth), BF16),
        grid_spec=pltpu.PrefetchScalarGridSpec(
            num_scalar_prefetch=2,
            grid=(1,),
            in_specs=[whole(band, breadth), whole(band, breadth)],
            out_specs=whole(band + more, breadth),
        ),
        compiler_params=params(),
        name="pack_roots",
    )(me, owner, left_root, right_root)


def place_packed(pieces, refs, numbers, half_l, half_r, band, breadth):
    tiles = breadth // TILE
    quarter = tiles // 4
    low = lower_half(TILE)
    zeros = jnp.zeros((TILE, PAIR), BF16)
    for offset, number in numbers.items():
        parts = [(first, ref) for (place, first, _), ref in zip(pieces, refs) if place == offset]
        more = max(first + ref.shape[0] for first, ref in parts) - band

        def rows_at(row, end, pairs):
            found = []
            for first, ref in parts:
                top, bottom = max(row, first), min(end, first + ref.shape[0])
                if top < bottom:
                    found.append(ref[top - first : bottom - first, pairs].astype(F32))
            return jnp.concatenate(found, 0) if len(found) > 1 else found[0]

        slot = jnp.int32(0)
        for row in range(0, band, TILE):
            tile = (number * (band // TILE) + row // TILE) & (tiles - 1)
            odd, pair = tile & 1, tile >> 1
            at = pl.ds(pl.multiple_of(number * band + row, TILE), TILE)
            here = meets(tile, tiles)
            both = jnp.concatenate(
                [
                    rows_at(band, band + more, lanes(slot * (TILE // more) + i, breadth))
                    for i in range(TILE // more)
                ],
                0,
            )
            slot = slot + here.astype(jnp.int32)
            other = swapped(both)
            late = low & (odd == 1)
            mine = (low == (odd == 0)) & here
            for start, half, value in (
                (0, half_l, jnp.where(odd == 1, other, both)),
                (quarter, half_r, jnp.where(odd == 1, both, other)),
            ):
                mixed = rows_at(row, row + TILE, slice(start * PAIR, (start + 1) * PAIR))
                half[at, lanes(pair, breadth)] = jnp.where(late, 0.0, mixed).astype(BF16)
                end = jnp.where(mine, value, jnp.where(late, mixed, 0.0))
                half[at, lanes(pair + quarter, breadth)] = end.astype(BF16)
                for i in range(1, quarter):
                    some = rows_at(row, row + TILE, slice((start + i) * PAIR, (start + i + 1) * PAIR))
                    half[at, lanes(pair + i, breadth)] = some.astype(BF16)
                    half[at, lanes(pair + quarter + i, breadth)] = zeros


def add_send(me, partial, arrived, distance, n, first, *after):
    band, breadth = partial.shape[1] // n, partial.shape[2]
    rows = arrived.shape[0]

    def kernel(me_ref, own_ref, a_ref, *refs):
        out_ref = refs[-1]
        if rows == band:
            out_ref[...] = (own_ref[0].astype(F32) + a_ref[...].astype(F32)).astype(BF16)
        else:
            got, other = slice(first, first + rows), slice(rows - first, band - first)
            out_ref[got] = (own_ref[0, got].astype(F32) + a_ref[...].astype(F32)).astype(BF16)
            out_ref[other] = own_ref[0, other]

    return pl.pallas_call(
        kernel,
        out_shape=jax.ShapeDtypeStruct((band, breadth), BF16),
        grid_spec=pltpu.PrefetchScalarGridSpec(
            num_scalar_prefetch=1,
            grid=(1,),
            in_specs=[
                pl.BlockSpec((1, band, breadth), lambda i, m: (0, away(m[0], distance, n), 0)),
                whole(rows, breadth),
            ]
            + [pl.BlockSpec(memory_space=pl.ANY)] * len(after),
            out_specs=whole(band, breadth),
        ),
        compiler_params=params(),
        name="add_send",
    )(me, partial, arrived, *after)


def add_own(me, partial, right, left, n, *after):
    band, breadth = partial.shape[1] // n, partial.shape[2]

    def kernel(me_ref, own_ref, r_ref, l_ref, *refs):
        out_ref = refs[-1]
        total = own_ref[0].astype(F32) + r_ref[...].astype(F32) + l_ref[...].astype(F32)
        out_ref[...] = total.astype(BF16)

    return pl.pallas_call(
        kernel,
        out_shape=jax.ShapeDtypeStruct((band, breadth), BF16),
        grid_spec=pltpu.PrefetchScalarGridSpec(
            num_scalar_prefetch=1,
            grid=(1,),
            in_specs=[
                pl.BlockSpec((1, band, breadth), lambda i, m: (0, m[0], 0)),
                whole(band, breadth),
                whole(band, breadth),
            ]
            + [pl.BlockSpec(memory_space=pl.ANY)] * len(after),
            out_specs=whole(band, breadth),
        ),
        compiler_params=params(),
        name="add_own",
    )(me, partial, right, left, *after)


def unpack_roots(me, owner, pieces, stacked, breadth, n):
    band = stacked // n
    tiles = breadth // TILE
    nblocks = stacked // breadth

    def kernel(me_ref, owner_ref, *refs):
        refs, (left_ref, right_ref, half_l, half_r, table, sem) = refs[: len(pieces)], refs[len(pieces) :]
        copy = pltpu.make_async_copy(owner_ref, table, sem)
        copy.start()
        shift = TILE.bit_length() - 1
        down = lax.broadcasted_iota(jnp.int32, (breadth, breadth), 0) >> shift
        over = lax.broadcasted_iota(jnp.int32, (breadth, breadth), 1) >> shift
        apart = over - down + jnp.where(over < down, tiles, 0)
        mirrored = (apart > 0) & (apart <= tiles // 2)
        copy.wait()
        numbers = {o: band_of(table, away(me_ref[0], o, n), n) for o in sorted({p[0] for p in pieces})}
        place_packed(pieces, refs, numbers, half_l, half_r, band, breadth)
        for half, out in ((half_r, right_ref), (half_l, left_ref)):
            for b in range(nblocks):
                rows = slice(b * breadth, (b + 1) * breadth)
                upper = half[rows]
                out[rows] = upper + jnp.where(mirrored, upper, jnp.zeros_like(upper)).T

    out = jax.ShapeDtypeStruct((stacked, breadth), BF16)
    return pl.pallas_call(
        kernel,
        out_shape=(out, out),
        grid_spec=pltpu.PrefetchScalarGridSpec(
            num_scalar_prefetch=1,
            grid=(1,),
            in_specs=[pl.BlockSpec(memory_space=pl.ANY)] + [whole(*x.shape) for _, _, x in pieces],
            out_specs=(whole(stacked, breadth), whole(stacked, breadth)),
            scratch_shapes=[pltpu.VMEM((stacked, breadth), BF16)] * 2
            + [pltpu.SMEM((n,), jnp.int32), pltpu.SemaphoreType.DMA],
        ),
        compiler_params=params(),
        name="unpack_roots",
    )(me, owner, *[x for _, _, x in pieces])


def begin(me, pieces, left_root, right_root, n):
    stacked, breadth = left_root.shape
    band = stacked // n
    nblocks = stacked // breadth

    def kernel(me_ref, *refs):
        parts, refs = refs[: len(pieces)], refs[len(pieces) :]
        lroot, rroot, dir_ref, grad, rest_ref = refs
        for (offset, first, _), ref in zip(pieces, parts):
            place = away(me_ref[0], offset, n) * band + first
            grad[pl.ds(pl.multiple_of(place, CHUNK), ref.shape[0]), :] = ref[...]
        start = away(me_ref[0], n // 2, n) * band
        grad[pl.ds(pl.multiple_of(start, CHUNK), band), :] = jnp.zeros((band, breadth), BF16)
        for b in range(nblocks):
            rows = slice(b * breadth, (b + 1) * breadth)
            mixed = jnp.dot(grad[rows], rroot[rows], preferred_element_type=F32).astype(BF16)
            block = jnp.dot(lroot[rows], mixed, preferred_element_type=F32)
            dir_ref[rows] = block.astype(BF16)
            for slot, at in enumerate((start, start + band - 1)):

                @pl.when(at >> (breadth.bit_length() - 1) == b)
                def _():
                    rest_ref[slot] = block

    return pl.pallas_call(
        kernel,
        out_shape=(
            jax.ShapeDtypeStruct((stacked, breadth), BF16),
            jax.ShapeDtypeStruct((stacked, breadth), BF16),
            jax.ShapeDtypeStruct((2, breadth, breadth), F32),
        ),
        grid_spec=pltpu.PrefetchScalarGridSpec(
            num_scalar_prefetch=1,
            grid=(1,),
            in_specs=[whole(*x.shape) for _, _, x in pieces] + [whole(stacked, breadth)] * 2,
            out_specs=(
                whole(stacked, breadth),
                whole(stacked, breadth),
                whole(2, breadth, breadth),
            ),
        ),
        compiler_params=params(),
        name="begin",
    )(me, *[x for _, _, x in pieces], left_root, right_root)


def finish(me, owner, pieces, directions, grad, rest, left_root, right_root, left_factor, right_factor, n):
    stacked, breadth = left_root.shape
    band = stacked // n
    nblocks = stacked // breadth

    def kernel(me_ref, owner_ref, *refs):
        parts, refs = refs[: len(pieces)], refs[len(pieces) :]
        part_ref, grad_ref, rest_ref, lroot, rroot, lfac, rfac, *refs = refs
        dir_ref, lout_ref, rout_ref, late, block, lout, rout, table, sems = refs
        lookup = pltpu.make_async_copy(owner_ref, table, sems.at[4 + nblocks])
        lookup.start()
        far = away(me_ref[0], n // 2, n) * band
        for (_, first, _), ref in zip(pieces, parts):
            late[first : first + ref.shape[0]] = ref[...]
        shift = breadth.bit_length() - 1
        row = (far + lax.broadcasted_iota(jnp.int32, (band, breadth), 0)) >> shift
        there = pl.ds(pl.multiple_of(far, CHUNK), band)
        first_block = far >> shift
        last_block = (far + band - 1) >> shift

        def span(number):
            return pl.ds(pl.multiple_of(number * breadth, breadth), breadth)

        def copy(slot, number):
            return pltpu.make_async_copy(block.at[slot], dir_ref.at[span(number)], sems.at[slot])

        def keep(b):
            rows = slice(b * breadth, (b + 1) * breadth)
            return pltpu.make_async_copy(part_ref.at[rows], dir_ref.at[rows], sems.at[4 + b])

        for b in range(nblocks):

            @pl.when((first_block != b) & (last_block != b))
            def _():
                keep(b).start()

        def complete(slot, number):
            some = jnp.where(row == number, late[...].astype(F32), 0.0).astype(BF16)
            mixed = jnp.dot(some, rroot[span(number), :], preferred_element_type=F32).astype(BF16)
            more = lax.dot_general(lroot[there, :], mixed, TN, preferred_element_type=F32)
            block[slot] = (rest_ref[slot] + more).astype(BF16)
            copy(slot, number).start()

        complete(0, first_block)

        @pl.when(last_block != first_block)
        def _():
            complete(1, last_block)

        lookup.wait()
        start = band_of(table, me_ref[0], n) * band
        grad_ref[there, :] = late[...]
        mine = grad_ref[pl.ds(pl.multiple_of(start, CHUNK), band), :]
        own_first = start >> shift
        own_last = (start + band - 1) >> shift
        own_row = start + lax.broadcasted_iota(jnp.int32, (band, breadth), 0)
        column = lax.broadcasted_iota(jnp.int32, (band, breadth), 1)

        def left_term(number):
            return lax.dot_general(mine, grad_ref[span(number), :], NT, preferred_element_type=F32)

        def right_term(number):
            g = grad_ref[span(number), :]
            pick = (own_row - number * breadth == column).astype(BF16)
            turned = lax.dot_general(pick, g, NT, preferred_element_type=F32).astype(BF16)
            return jnp.dot(turned, g, preferred_element_type=F32)

        later = own_row >= own_last * breadth
        outs = []
        for slot, (term, fac, out, ref) in enumerate(
            ((left_term, lfac, lout, lout_ref), (right_term, rfac, rout, rout_ref))
        ):
            out[...] = BETA * fac[...] + (1.0 - BETA) * term(own_first)

            @pl.when(own_last != own_first)
            def _():
                new = BETA * fac[...] + (1.0 - BETA) * term(own_last)
                out[...] = jnp.where(later, new, out[...])

            outs.append(pltpu.make_async_copy(out, ref, sems.at[2 + slot]))
            outs[-1].start()
        copy(0, first_block).wait()

        @pl.when(last_block != first_block)
        def _():
            copy(1, last_block).wait()

        for b in range(nblocks):

            @pl.when((first_block != b) & (last_block != b))
            def _():
                keep(b).wait()

        for out in outs:
            out.wait()

    own = jax.ShapeDtypeStruct((band, breadth), F32)
    return pl.pallas_call(
        kernel,
        out_shape=(jax.ShapeDtypeStruct((stacked, breadth), BF16), own, own),
        grid_spec=pltpu.PrefetchScalarGridSpec(
            num_scalar_prefetch=1,
            grid=(1,),
            in_specs=[pl.BlockSpec(memory_space=pl.ANY)]
            + [whole(*x.shape) for _, _, x in pieces]
            + [whole(stacked, breadth)] * 2
            + [whole(2, breadth, breadth)]
            + [whole(stacked, breadth)] * 2
            + [whole(band, breadth)] * 2,
            out_specs=[pl.BlockSpec(memory_space=pl.ANY)] * 3,
            scratch_shapes=[
                pltpu.VMEM((band, breadth), BF16),
                pltpu.VMEM((2, breadth, breadth), BF16),
                pltpu.VMEM((band, breadth), F32),
                pltpu.VMEM((band, breadth), F32),
                pltpu.SMEM((n,), jnp.int32),
                pltpu.SemaphoreType.DMA((5 + nblocks,)),
            ],
        ),
        compiler_params=params(),
        name="finish",
    )(
        me,
        owner,
        *[x for _, _, x in pieces],
        directions,
        grad,
        rest,
        left_root,
        right_root,
        left_factor,
        right_factor,
    )


def ring(n, partial_grads, band_owner, left_factor, right_factor, left_root, right_root):
    stacked, breadth = partial_grads.shape[1:]
    band = stacked // n
    half = band // 2
    me = lax.axis_index("dp").astype(jnp.int32).reshape(1)
    order = [2 * q for q in range(n // 2)] + [2 * (n - 1 - q) + 1 for q in range(n // 2, n)]
    onward = [(order[q], order[(q + 1) % n]) for q in range(n)]
    backward = [(b, a) for a, b in onward]

    def send_right(x):
        return lax.ppermute(x, "dp", onward)

    def send_left(x):
        return lax.ppermute(x, "dp", backward)

    def gather(own, parts):
        rows = own.shape[0] // 2
        pieces = [(0, 0, own)]
        if parts == 1:
            right, left = own, own
            for hop in range(1, n // 2):
                right, left = send_right(right), send_left(left)
                pieces += [(-hop, 0, right), (hop, 0, left)]
            right, left = send_right(right[:rows]), send_left(left[rows:])
        else:
            upper, lower = own[:rows], own[rows:]
            ways = [upper, upper, lower, lower]
            for hop in range(1, n // 2):
                ways = [
                    send_left(ways[3]),
                    send_right(ways[2]),
                    send_left(ways[1]),
                    send_right(ways[0]),
                ][::-1]
                pieces += [(-hop, 0, ways[0]), (hop, 0, ways[1])]
                pieces += [(-hop, rows, ways[2]), (hop, rows, ways[3])]
            right, left = send_right(ways[0]), send_left(ways[3])
        return pieces + [(n // 2, 0, right), (n // 2, rows, left)]

    right, left = first_sends(me, partial_grads, n)
    packed = pack_roots(me, band_owner, left_root, right_root, n)
    right, left = send_right(right), send_left(left)
    root_pieces = gather(packed, 1)
    for distance in range(n // 2 - 1, 0, -1):
        right = add_send(me, partial_grads, right, distance, n, 0)
        left = add_send(me, partial_grads, left, -distance, n, half if left.shape[0] == half else 0)
        right, left = send_right(right), send_left(left)
    roots = unpack_roots(me, band_owner, root_pieces, stacked, breadth, n)
    own = add_own(me, partial_grads, right, left, n)
    pieces = gather(own, GRAD_PARTS)
    begun = begin(me, pieces[:-2], *roots, n)
    return finish(me, band_owner, pieces[-2:], *begun, *roots, left_factor, right_factor, n)


def shards(n, partial_grads, *rest):
    stacked, breadth = partial_grads.shape[1:]
    band = stacked // n
    fits = band % TILE == 0 and breadth % (4 * TILE) == 0 and breadth & (breadth - 1) == 0
    if fits:
        more = slots_of(n, band, breadth // TILE) * TILE * PAIR // breadth
        fits = more > 0 and TILE % more == 0 and (band + more) % 32 == 0
    if 4 <= n <= 16 and n % 2 == 0 and fits:
        return ring(n, partial_grads, *rest)
    return general(partial_grads, *rest)


def solution(mesh):
    placed = (P("dp", None, "mp"), P(), P("dp", "mp"), P("dp", "mp"), P("dp", "mp"), P("dp", "mp"))
    return jax.shard_map(
        functools.partial(shards, mesh.shape["dp"]),
        mesh=mesh,
        in_specs=placed,
        out_specs=(P(None, "mp"), P("dp", "mp"), P("dp", "mp")),
        check_vma=False,
    )
```

```python
import functools

import jax
import jax.numpy as jnp
from jax import lax
from jax.experimental import pallas as pl
from jax.experimental.pallas import tpu as pltpu
from jax.sharding import PartitionSpec as P

BETA = 0.95
TILE = 64
CHUNK = 32
GRAD_PARTS = 2
F32 = jnp.float32
BF16 = jnp.bfloat16
NT = (((1,), (1,)), ((), ()))
TN = (((0,), (0,)), ((), ()))
VMEM_LIMIT = 40 * 1024 * 1024


def against(band_rows, whole_rows, select):
    nblocks = select.shape[1]
    breadth = whole_rows.shape[1]
    blocks = whole_rows.reshape(nblocks, breadth, breadth)
    products = jnp.einsum("rk,bck->rbc", band_rows, blocks, preferred_element_type=jnp.float32)
    return jnp.sum(select[:, :, None] * products, axis=1)


def to_band_order(gathered, owners, members):
    shaped = gathered.reshape(members, -1, gathered.shape[1])
    return jnp.take(shaped, owners, axis=0).reshape(gathered.shape)


def general(partial_grads, band_owner, left_factor, right_factor, left_root, right_root):
    members = lax.axis_size("dp")
    band_size = left_factor.shape[0]
    breadth = left_factor.shape[1]
    stacked = partial_grads.shape[1]
    nblocks = stacked // breadth
    devices = jnp.arange(members, dtype=jnp.int32)
    inverse = jnp.sum(
        jnp.where(band_owner[None, :] == devices[:, None], devices[None, :], 0), axis=1
    )
    own_band = inverse[lax.axis_index("dp")]
    partial_value = partial_grads[0]
    even_rows = lax.psum_scatter(
        partial_value.astype(jnp.float32), "dp", scatter_dimension=0, tiled=True
    ).astype(jnp.bfloat16)
    grad_full = lax.all_gather(even_rows, "dp", axis=0, tiled=True)
    grad_rows = lax.dynamic_slice_in_dim(grad_full, own_band * band_size, band_size, 0)
    global_rows = own_band * band_size + jnp.arange(band_size, dtype=jnp.int32)
    block_ids = global_rows // breadth
    within = global_rows % breadth
    block_range = jnp.arange(nblocks, dtype=jnp.int32)
    select = (block_ids[:, None] == block_range[None, :]).astype(jnp.float32)
    left_term = against(grad_rows, grad_full, select)
    left_updated = BETA * left_factor + (1.0 - BETA) * left_term
    column_range = jnp.arange(breadth, dtype=jnp.int32)
    onehot = (
        (block_range[:, None, None] == block_ids[None, None, :])
        & (column_range[None, :, None] == within[None, None, :])
    ).astype(jnp.bfloat16)
    blocks = grad_full.reshape(nblocks, breadth, breadth)
    columns = jnp.einsum("bkc,bcr->kr", blocks, onehot, preferred_element_type=jnp.float32).astype(
        jnp.bfloat16
    )
    right_products = jnp.einsum("kr,bkc->rbc", columns, blocks, preferred_element_type=jnp.float32)
    right_term = jnp.sum(select[:, :, None] * right_products, axis=1)
    right_updated = BETA * right_factor + (1.0 - BETA) * right_term
    mixed_rows = against(right_root, grad_full, select).astype(jnp.bfloat16)
    mixed_full = to_band_order(
        lax.all_gather(mixed_rows, "dp", axis=0, tiled=True), band_owner, members
    )
    direction_rows = against(left_root, mixed_full, select).astype(jnp.bfloat16)
    direction = to_band_order(
        lax.all_gather(direction_rows, "dp", axis=0, tiled=True), band_owner, members
    )
    return (direction, left_updated, right_updated)


def seat_of(device, n):
    return jnp.where((device & 1) == 0, device >> 1, n - ((device + 1) >> 1))


def device_at(seat, n):
    seat = jnp.where(seat < 0, seat + n, seat)
    seat = jnp.where(seat >= n, seat - n, seat)
    return jnp.where(seat < n // 2, 2 * seat, 2 * (n - 1 - seat) + 1)


def away(me, offset, n):
    return device_at(seat_of(me, n) + offset, n)


def band_of(owner_ref, device, n):
    order = lax.broadcasted_iota(jnp.int32, (1, n), 1)
    hit = owner_ref[...] == device
    return jnp.sum(jnp.where(hit, order, 0).astype(F32)).astype(jnp.int32)


def whole(*shape):
    return pl.BlockSpec(shape, lambda i, *_: (0,) * len(shape))


def params(limit=VMEM_LIMIT):
    return pltpu.CompilerParams(vmem_limit_bytes=limit)


PAIR = 2 * TILE


def meets(tile, tiles):
    half, quarter = tiles // 2, tiles // 4
    return ((tile < half) & (tile != quarter)) | (tile == half + quarter)


def slots_of(n, band, tiles):
    rows = band // TILE
    return max(sum(meets((k * rows + t) % tiles, tiles) for t in range(rows)) for k in range(n))


def lanes(pair, breadth):
    return pl.ds(pl.multiple_of((pair & (breadth // PAIR - 1)) * PAIR, PAIR), PAIR)


def lower_half(rows):
    return lax.broadcasted_iota(jnp.int32, (rows, PAIR), 1) < TILE


def swapped(x):
    return pltpu.roll(x, TILE, 1)


def first_sends(me, partial, n):
    breadth = partial.shape[2]
    band = partial.shape[1] // n
    half = band // 2

    def kernel(me_ref, far_ref, right_ref, left_ref):
        right_ref[...] = far_ref[0, :half]
        left_ref[...] = far_ref[0, half:]

    sent = jax.ShapeDtypeStruct((half, breadth), BF16)
    return pl.pallas_call(
        kernel,
        out_shape=(sent, sent),
        grid_spec=pltpu.PrefetchScalarGridSpec(
            num_scalar_prefetch=1,
            grid=(1,),
            in_specs=[
                pl.BlockSpec((1, band, breadth), lambda i, m: (0, away(m[0], n // 2, n), 0)),
            ],
            out_specs=(whole(half, breadth), whole(half, breadth)),
        ),
        compiler_params=params(),
        name="first_sends",
    )(me, partial)


def pack_roots(me, owner, left_root, right_root, n):
    band, breadth = left_root.shape
    tiles = breadth // TILE
    quarter = tiles // 4
    more = slots_of(n, band, tiles) * TILE * PAIR // breadth

    def kernel(me_ref, owner_ref, l_ref, r_ref, out_ref):
        number = band_of(owner_ref, me_ref[0], n)
        low = lower_half(TILE)
        out_ref[band:] = jnp.zeros((more, breadth), BF16)
        slot = jnp.int32(0)
        for row in range(0, band, TILE):
            tile = (number * (band // TILE) + row // TILE) & (tiles - 1)
            odd, pair = tile & 1, tile >> 1
            rows = slice(row, row + TILE)
            last = lanes(pair + quarter, breadth)
            for at, ref in ((0, l_ref), (quarter, r_ref)):
                start = ref[rows, lanes(pair, breadth)].astype(F32)
                end = ref[rows, last].astype(F32)
                mixed = jnp.where(low & (odd == 1), end, start).astype(BF16)
                out_ref[rows, at * PAIR : (at + 1) * PAIR] = mixed
                for i in range(1, quarter):
                    out_ref[rows, (at + i) * PAIR : (at + i + 1) * PAIR] = ref[rows, lanes(pair + i, breadth)]
            here = meets(tile, tiles)

            @pl.when(here)
            def _():
                left, right = l_ref[rows, last].astype(F32), r_ref[rows, last].astype(F32)
                left = jnp.where(odd == 1, swapped(left), left)
                right = jnp.where(odd == 1, right, swapped(right))
                both = jnp.where(low, left, right).astype(BF16)
                for i in range(TILE // more):
                    place = lanes(slot * (TILE // more) + i, breadth)
                    out_ref[band : band + more, place] = both[i * more : (i + 1) * more]

            slot = slot + here.astype(jnp.int32)

    return pl.pallas_call(
        kernel,
        out_shape=jax.ShapeDtypeStruct((band + more, breadth), BF16),
        grid_spec=pltpu.PrefetchScalarGridSpec(
            num_scalar_prefetch=1,
            grid=(1,),
            in_specs=[whole(1, n), whole(band, breadth), whole(band, breadth)],
            out_specs=whole(band + more, breadth),
        ),
        compiler_params=params(),
        name="pack_roots",
    )(me, owner, left_root, right_root)


def place_packed(pieces, refs, numbers, half_l, half_r, band, breadth):
    tiles = breadth // TILE
    quarter = tiles // 4
    low = lower_half(TILE)
    for offset, number in numbers.items():
        parts = [(first, ref) for (place, first, _), ref in zip(pieces, refs) if place == offset]
        more = max(first + ref.shape[0] for first, ref in parts) - band

        def rows_at(row, end, pairs):
            found = []
            for first, ref in parts:
                top, bottom = max(row, first), min(end, first + ref.shape[0])
                if top < bottom:
                    found.append(ref[top - first : bottom - first, pairs].astype(F32))
            return jnp.concatenate(found, 0) if len(found) > 1 else found[0]

        slot = jnp.int32(0)
        for row in range(0, band, TILE):
            tile = (number * (band // TILE) + row // TILE) & (tiles - 1)
            odd, pair = tile & 1, tile >> 1
            at = pl.ds(pl.multiple_of(number * band + row, TILE), TILE)
            here = meets(tile, tiles)
            both = jnp.concatenate(
                [
                    rows_at(band, band + more, lanes(slot * (TILE // more) + i, breadth))
                    for i in range(TILE // more)
                ],
                0,
            )
            slot = slot + here.astype(jnp.int32)
            other = swapped(both)
            late = low & (odd == 1)
            mine = (low == (odd == 0)) & here
            for start, half, value in (
                (0, half_l, jnp.where(odd == 1, other, both)),
                (quarter, half_r, jnp.where(odd == 1, both, other)),
            ):
                mixed = rows_at(row, row + TILE, slice(start * PAIR, (start + 1) * PAIR))
                half[at, lanes(pair, breadth)] = jnp.where(late, 0.0, mixed).astype(BF16)
                end = jnp.where(mine, value, jnp.where(late, mixed, 0.0))
                half[at, lanes(pair + quarter, breadth)] = end.astype(BF16)
                for i in range(1, quarter):
                    some = rows_at(row, row + TILE, slice((start + i) * PAIR, (start + i + 1) * PAIR))
                    half[at, lanes(pair + i, breadth)] = some.astype(BF16)


def add_send(me, partial, arrived, distance, n, first, *after):
    band, breadth = partial.shape[1] // n, partial.shape[2]
    rows = arrived.shape[0]

    def kernel(me_ref, own_ref, a_ref, *refs):
        out_ref = refs[-1]
        if rows == band:
            out_ref[...] = (own_ref[0].astype(F32) + a_ref[...].astype(F32)).astype(BF16)
        else:
            got, other = slice(first, first + rows), slice(rows - first, band - first)
            out_ref[got] = (own_ref[0, got].astype(F32) + a_ref[...].astype(F32)).astype(BF16)
            out_ref[other] = own_ref[0, other]

    return pl.pallas_call(
        kernel,
        out_shape=jax.ShapeDtypeStruct((band, breadth), BF16),
        grid_spec=pltpu.PrefetchScalarGridSpec(
            num_scalar_prefetch=1,
            grid=(1,),
            in_specs=[
                pl.BlockSpec((1, band, breadth), lambda i, m: (0, away(m[0], distance, n), 0)),
                whole(rows, breadth),
            ]
            + [pl.BlockSpec(memory_space=pl.ANY)] * len(after),
            out_specs=whole(band, breadth),
        ),
        compiler_params=params(),
        name="add_send",
    )(me, partial, arrived, *after)


def add_own(me, partial, right, left, n, *after):
    band, breadth = partial.shape[1] // n, partial.shape[2]

    def kernel(me_ref, own_ref, r_ref, l_ref, *refs):
        out_ref = refs[-1]
        total = own_ref[0].astype(F32) + r_ref[...].astype(F32) + l_ref[...].astype(F32)
        out_ref[...] = total.astype(BF16)

    return pl.pallas_call(
        kernel,
        out_shape=jax.ShapeDtypeStruct((band, breadth), BF16),
        grid_spec=pltpu.PrefetchScalarGridSpec(
            num_scalar_prefetch=1,
            grid=(1,),
            in_specs=[
                pl.BlockSpec((1, band, breadth), lambda i, m: (0, m[0], 0)),
                whole(band, breadth),
                whole(band, breadth),
            ]
            + [pl.BlockSpec(memory_space=pl.ANY)] * len(after),
            out_specs=whole(band, breadth),
        ),
        compiler_params=params(),
        name="add_own",
    )(me, partial, right, left, *after)


def unpack_roots(me, owner, pieces, stacked, breadth, n):
    band = stacked // n
    tiles = breadth // TILE
    nblocks = stacked // breadth

    def kernel(me_ref, owner_ref, *refs):
        refs, (left_ref, right_ref, half_l, half_r) = refs[: len(pieces)], refs[len(pieces) :]
        upper = lax.broadcasted_iota(jnp.int32, (PAIR, PAIR), 0) < TILE
        aside = upper & (lax.broadcasted_iota(jnp.int32, (PAIR, PAIR), 1) >= TILE)
        numbers = {}
        for offset in sorted({p[0] for p in pieces}):
            numbers[offset] = band_of(owner_ref, away(me_ref[0], offset, n), n)
        place_packed(pieces, refs, numbers, half_l, half_r, band, breadth)
        pairs = tiles // 2
        for half, out in ((half_r, right_ref), (half_l, left_ref)):
            for b in range(nblocks):

                def square(i, j):
                    top = b * breadth + i * PAIR
                    return slice(top, top + PAIR), slice(j * PAIR, (j + 1) * PAIR)

                for i in range(pairs):
                    for j in range(pairs):
                        apart = (i - j) % pairs
                        if apart == 0:
                            here = half[square(i, i)]
                            value = here + jnp.where(aside, here, jnp.zeros_like(here)).T
                        elif apart < pairs // 2:
                            value = half[square(j, i)].T
                        elif apart == pairs // 2:
                            value = half[square(i, j)] + half[square(j, i)].T
                        else:
                            value = half[square(i, j)]
                        out[square(i, j)] = value

    out = jax.ShapeDtypeStruct((stacked, breadth), BF16)
    return pl.pallas_call(
        kernel,
        out_shape=(out, out),
        grid_spec=pltpu.PrefetchScalarGridSpec(
            num_scalar_prefetch=1,
            grid=(1,),
            in_specs=[whole(1, n)] + [whole(*x.shape) for _, _, x in pieces],
            out_specs=(whole(stacked, breadth), whole(stacked, breadth)),
            scratch_shapes=[pltpu.VMEM((stacked, breadth), BF16)] * 2,
        ),
        compiler_params=params(),
        name="unpack_roots",
    )(me, owner, *[x for _, _, x in pieces])


def begin(me, pieces, left_root, right_root, n):
    stacked, breadth = left_root.shape
    band = stacked // n
    nblocks = stacked // breadth

    def kernel(me_ref, *refs):
        parts, refs = refs[: len(pieces)], refs[len(pieces) :]
        lroot, rroot, dir_ref, grad, rest_ref = refs
        for (offset, first, _), ref in zip(pieces, parts):
            place = away(me_ref[0], offset, n) * band + first
            grad[pl.ds(pl.multiple_of(place, CHUNK), ref.shape[0]), :] = ref[...]
        start = away(me_ref[0], n // 2, n) * band
        grad[pl.ds(pl.multiple_of(start, CHUNK), band), :] = jnp.zeros((band, breadth), BF16)
        for b in range(nblocks):
            rows = slice(b * breadth, (b + 1) * breadth)
            mixed = jnp.dot(grad[rows], rroot[rows], preferred_element_type=F32).astype(BF16)
            block = jnp.dot(lroot[rows], mixed, preferred_element_type=F32)
            dir_ref[rows] = block.astype(BF16)
            rest_ref[b] = block

    return pl.pallas_call(
        kernel,
        out_shape=(
            jax.ShapeDtypeStruct((stacked, breadth), BF16),
            jax.ShapeDtypeStruct((stacked, breadth), BF16),
            jax.ShapeDtypeStruct((nblocks, breadth, breadth), F32),
        ),
        grid_spec=pltpu.PrefetchScalarGridSpec(
            num_scalar_prefetch=1,
            grid=(1,),
            in_specs=[whole(*x.shape) for _, _, x in pieces] + [whole(stacked, breadth)] * 2,
            out_specs=(
                whole(stacked, breadth),
                whole(stacked, breadth),
                whole(nblocks, breadth, breadth),
            ),
        ),
        compiler_params=params(),
        name="begin",
    )(me, *[x for _, _, x in pieces], left_root, right_root)


def finish(me, owner, pieces, directions, grad, rest, left_root, right_root, left_factor, right_factor, n):
    stacked, breadth = left_root.shape
    band = stacked // n
    nblocks = stacked // breadth

    def kernel(me_ref, owner_ref, *refs):
        parts, refs = refs[: len(pieces)], refs[len(pieces) :]
        part_ref, grad_ref, rest_ref, lroot, rroot, lfac, rfac, *refs = refs
        dir_ref, lout_ref, rout_ref, late, block, lout, rout, sems = refs
        far = away(me_ref[0], n // 2, n) * band
        for (_, first, _), ref in zip(pieces, parts):
            late[first : first + ref.shape[0]] = ref[...]
        shift = breadth.bit_length() - 1
        row = (far + lax.broadcasted_iota(jnp.int32, (band, breadth), 0)) >> shift
        there = pl.ds(pl.multiple_of(far, CHUNK), band)
        first_block = far >> shift
        last_block = (far + band - 1) >> shift

        def span(number):
            return pl.ds(pl.multiple_of(number * breadth, breadth), breadth)

        def copy(slot, number):
            return pltpu.make_async_copy(block.at[slot], dir_ref.at[span(number)], sems.at[slot])

        def keep(b):
            rows = slice(b * breadth, (b + 1) * breadth)
            return pltpu.make_async_copy(part_ref.at[rows], dir_ref.at[rows], sems.at[4 + b])

        for b in range(nblocks):

            @pl.when((first_block != b) & (last_block != b))
            def _():
                keep(b).start()

        def complete(slot, number):
            some = jnp.where(row == number, late[...].astype(F32), 0.0).astype(BF16)
            mixed = jnp.dot(some, rroot[span(number), :], preferred_element_type=F32).astype(BF16)
            more = lax.dot_general(lroot[there, :], mixed, TN, preferred_element_type=F32)
            block[slot] = (rest_ref[number] + more).astype(BF16)

        start = band_of(owner_ref, me_ref[0], n) * band
        grad_ref[there, :] = late[...]
        mine = grad_ref[pl.ds(pl.multiple_of(start, CHUNK), band), :]
        own_first = start >> shift
        own_last = (start + band - 1) >> shift
        own_row = start + lax.broadcasted_iota(jnp.int32, (band, breadth), 0)
        column = lax.broadcasted_iota(jnp.int32, (band, breadth), 1)

        def renewed(number):
            g = grad_ref[span(number), :]
            left = lax.dot_general(mine, g, NT, preferred_element_type=F32)
            pick = (own_row - number * breadth == column).astype(BF16)
            turned = lax.dot_general(pick, g, NT, preferred_element_type=F32).astype(BF16)
            right = jnp.dot(turned, g, preferred_element_type=F32)
            return BETA * lfac[...] + (1.0 - BETA) * left, BETA * rfac[...] + (1.0 - BETA) * right

        complete(0, first_block)
        lout[...], rout[...] = renewed(own_first)
        copy(0, first_block).start()

        @pl.when(last_block != first_block)
        def _():
            complete(1, last_block)
            copy(1, last_block).start()

        @pl.when(own_last != own_first)
        def _():
            later = own_row >= own_last * breadth
            left, right = renewed(own_last)
            lout[...] = jnp.where(later, left, lout[...])
            rout[...] = jnp.where(later, right, rout[...])

        outs = []
        for slot, (out, ref) in enumerate(((lout, lout_ref), (rout, rout_ref))):
            outs.append(pltpu.make_async_copy(out, ref, sems.at[2 + slot]))
            outs[-1].start()
        copy(0, first_block).wait()

        @pl.when(last_block != first_block)
        def _():
            copy(1, last_block).wait()

        for b in range(nblocks):

            @pl.when((first_block != b) & (last_block != b))
            def _():
                keep(b).wait()

        for out in outs:
            out.wait()

    own = jax.ShapeDtypeStruct((band, breadth), F32)
    return pl.pallas_call(
        kernel,
        out_shape=(jax.ShapeDtypeStruct((stacked, breadth), BF16), own, own),
        grid_spec=pltpu.PrefetchScalarGridSpec(
            num_scalar_prefetch=1,
            grid=(1,),
            in_specs=[whole(1, n)]
            + [whole(*x.shape) for _, _, x in pieces]
            + [whole(stacked, breadth)] * 2
            + [whole(nblocks, breadth, breadth)]
            + [whole(stacked, breadth)] * 2
            + [whole(band, breadth)] * 2,
            out_specs=[pl.BlockSpec(memory_space=pl.ANY)] * 3,
            scratch_shapes=[
                pltpu.VMEM((band, breadth), BF16),
                pltpu.VMEM((2, breadth, breadth), BF16),
                pltpu.VMEM((band, breadth), F32),
                pltpu.VMEM((band, breadth), F32),
                pltpu.SemaphoreType.DMA((4 + nblocks,)),
            ],
        ),
        compiler_params=params(),
        name="finish",
    )(
        me,
        owner,
        *[x for _, _, x in pieces],
        directions,
        grad,
        rest,
        left_root,
        right_root,
        left_factor,
        right_factor,
    )


def ring(n, partial_grads, band_owner, left_factor, right_factor, left_root, right_root):
    stacked, breadth = partial_grads.shape[1:]
    band = stacked // n
    half = band // 2
    me = lax.axis_index("dp").astype(jnp.int32).reshape(1)
    owner = band_owner.reshape(1, n)
    order = [2 * q for q in range(n // 2)] + [2 * (n - 1 - q) + 1 for q in range(n // 2, n)]
    onward = [(order[q], order[(q + 1) % n]) for q in range(n)]
    backward = [(b, a) for a, b in onward]

    def send_right(x):
        return lax.ppermute(x, "dp", onward)

    def send_left(x):
        return lax.ppermute(x, "dp", backward)

    def gather(own, parts):
        rows = own.shape[0] // 2
        pieces = [(0, 0, own)]
        if parts == 1:
            right, left = own, own
            for hop in range(1, n // 2):
                right, left = send_right(right), send_left(left)
                pieces += [(-hop, 0, right), (hop, 0, left)]
            right, left = send_right(right[:rows]), send_left(left[rows:])
        else:
            upper, lower = own[:rows], own[rows:]
            ways = [upper, upper, lower, lower]
            for hop in range(1, n // 2):
                ways = [
                    send_left(ways[3]),
                    send_right(ways[2]),
                    send_left(ways[1]),
                    send_right(ways[0]),
                ][::-1]
                pieces += [(-hop, 0, ways[0]), (hop, 0, ways[1])]
                pieces += [(-hop, rows, ways[2]), (hop, rows, ways[3])]
            right, left = send_right(ways[0]), send_left(ways[3])
        return pieces + [(n // 2, 0, right), (n // 2, rows, left)]

    right, left = first_sends(me, partial_grads, n)
    packed = pack_roots(me, owner, left_root, right_root, n)
    right, left = send_right(right), send_left(left)
    root_pieces = gather(packed, 1)
    for distance in range(n // 2 - 1, 0, -1):
        right = add_send(me, partial_grads, right, distance, n, 0)
        left = add_send(me, partial_grads, left, -distance, n, half if left.shape[0] == half else 0)
        right, left = send_right(right), send_left(left)
    roots = unpack_roots(me, owner, root_pieces, stacked, breadth, n)
    own = add_own(me, partial_grads, right, left, n)
    pieces = gather(own, GRAD_PARTS)
    begun = begin(me, pieces[:-2], *roots, n)
    return finish(me, owner, pieces[-2:], *begun, *roots, left_factor, right_factor, n)


def shards(n, partial_grads, *rest):
    stacked, breadth = partial_grads.shape[1:]
    band = stacked // n
    fits = band % TILE == 0 and breadth % (4 * TILE) == 0 and breadth & (breadth - 1) == 0
    if fits:
        more = slots_of(n, band, breadth // TILE) * TILE * PAIR // breadth
        fits = more > 0 and TILE % more == 0 and (band + more) % 32 == 0
    if 4 <= n <= 16 and n % 2 == 0 and fits:
        return ring(n, partial_grads, *rest)
    return general(partial_grads, *rest)


def solution(mesh):
    placed = (P("dp", None, "mp"), P(), P("dp", "mp"), P("dp", "mp"), P("dp", "mp"), P("dp", "mp"))
    return jax.shard_map(
        functools.partial(shards, mesh.shape["dp"]),
        mesh=mesh,
        in_specs=placed,
        out_specs=(P(None, "mp"), P("dp", "mp"), P("dp", "mp")),
        check_vma=False,
    )
```

```python
import functools

import jax
import jax.numpy as jnp
from jax import lax
from jax.experimental import pallas as pl
from jax.experimental.pallas import tpu as pltpu
from jax.sharding import PartitionSpec as P

BETA = 0.95
TILE = 64
CHUNK = 32
GRAD_PARTS = 2
F32 = jnp.float32
BF16 = jnp.bfloat16
NT = (((1,), (1,)), ((), ()))
TN = (((0,), (0,)), ((), ()))
VMEM_LIMIT = 40 * 1024 * 1024


def against(band_rows, whole_rows, select):
    nblocks = select.shape[1]
    breadth = whole_rows.shape[1]
    blocks = whole_rows.reshape(nblocks, breadth, breadth)
    products = jnp.einsum("rk,bck->rbc", band_rows, blocks, preferred_element_type=jnp.float32)
    return jnp.sum(select[:, :, None] * products, axis=1)


def to_band_order(gathered, owners, members):
    shaped = gathered.reshape(members, -1, gathered.shape[1])
    return jnp.take(shaped, owners, axis=0).reshape(gathered.shape)


def general(partial_grads, band_owner, left_factor, right_factor, left_root, right_root):
    members = lax.axis_size("dp")
    band_size = left_factor.shape[0]
    breadth = left_factor.shape[1]
    stacked = partial_grads.shape[1]
    nblocks = stacked // breadth
    devices = jnp.arange(members, dtype=jnp.int32)
    inverse = jnp.sum(
        jnp.where(band_owner[None, :] == devices[:, None], devices[None, :], 0), axis=1
    )
    own_band = inverse[lax.axis_index("dp")]
    partial_value = partial_grads[0]
    even_rows = lax.psum_scatter(
        partial_value.astype(jnp.float32), "dp", scatter_dimension=0, tiled=True
    ).astype(jnp.bfloat16)
    grad_full = lax.all_gather(even_rows, "dp", axis=0, tiled=True)
    grad_rows = lax.dynamic_slice_in_dim(grad_full, own_band * band_size, band_size, 0)
    global_rows = own_band * band_size + jnp.arange(band_size, dtype=jnp.int32)
    block_ids = global_rows // breadth
    within = global_rows % breadth
    block_range = jnp.arange(nblocks, dtype=jnp.int32)
    select = (block_ids[:, None] == block_range[None, :]).astype(jnp.float32)
    left_term = against(grad_rows, grad_full, select)
    left_updated = BETA * left_factor + (1.0 - BETA) * left_term
    column_range = jnp.arange(breadth, dtype=jnp.int32)
    onehot = (
        (block_range[:, None, None] == block_ids[None, None, :])
        & (column_range[None, :, None] == within[None, None, :])
    ).astype(jnp.bfloat16)
    blocks = grad_full.reshape(nblocks, breadth, breadth)
    columns = jnp.einsum("bkc,bcr->kr", blocks, onehot, preferred_element_type=jnp.float32).astype(
        jnp.bfloat16
    )
    right_products = jnp.einsum("kr,bkc->rbc", columns, blocks, preferred_element_type=jnp.float32)
    right_term = jnp.sum(select[:, :, None] * right_products, axis=1)
    right_updated = BETA * right_factor + (1.0 - BETA) * right_term
    mixed_rows = against(right_root, grad_full, select).astype(jnp.bfloat16)
    mixed_full = to_band_order(
        lax.all_gather(mixed_rows, "dp", axis=0, tiled=True), band_owner, members
    )
    direction_rows = against(left_root, mixed_full, select).astype(jnp.bfloat16)
    direction = to_band_order(
        lax.all_gather(direction_rows, "dp", axis=0, tiled=True), band_owner, members
    )
    return (direction, left_updated, right_updated)


def seat_of(device, n):
    return jnp.where((device & 1) == 0, device >> 1, n - ((device + 1) >> 1))


def device_at(seat, n):
    seat = jnp.where(seat < 0, seat + n, seat)
    seat = jnp.where(seat >= n, seat - n, seat)
    return jnp.where(seat < n // 2, 2 * seat, 2 * (n - 1 - seat) + 1)


def away(me, offset, n):
    return device_at(seat_of(me, n) + offset, n)


def band_of(owner_ref, device, n):
    order = lax.broadcasted_iota(jnp.int32, (1, n), 1)
    hit = owner_ref[...] == device
    return jnp.sum(jnp.where(hit, order, 0).astype(F32)).astype(jnp.int32)


def whole(*shape):
    return pl.BlockSpec(shape, lambda i, *_: (0,) * len(shape))


def params(limit=VMEM_LIMIT):
    return pltpu.CompilerParams(vmem_limit_bytes=limit)


PAIR = 2 * TILE


def meets(tile, tiles):
    half, quarter = tiles // 2, tiles // 4
    return ((tile < half) & (tile != quarter)) | (tile == half + quarter)


def slots_of(n, band, tiles):
    rows = band // TILE
    return max(sum(meets((k * rows + t) % tiles, tiles) for t in range(rows)) for k in range(n))


def lanes(pair, breadth):
    return pl.ds(pl.multiple_of((pair & (breadth // PAIR - 1)) * PAIR, PAIR), PAIR)


def lower_half(rows):
    return lax.broadcasted_iota(jnp.int32, (rows, PAIR), 1) < TILE


def swapped(x):
    return pltpu.roll(x, TILE, 1)


def first_sends(me, partial, n):
    breadth = partial.shape[2]
    band = partial.shape[1] // n
    half = band // 2

    def kernel(me_ref, far_ref, right_ref, left_ref):
        right_ref[...] = far_ref[0, :half]
        left_ref[...] = far_ref[0, half:]

    sent = jax.ShapeDtypeStruct((half, breadth), BF16)
    return pl.pallas_call(
        kernel,
        out_shape=(sent, sent),
        grid_spec=pltpu.PrefetchScalarGridSpec(
            num_scalar_prefetch=1,
            grid=(1,),
            in_specs=[
                pl.BlockSpec((1, band, breadth), lambda i, m: (0, away(m[0], n // 2, n), 0)),
            ],
            out_specs=(whole(half, breadth), whole(half, breadth)),
        ),
        compiler_params=params(),
        name="first_sends",
    )(me, partial)


def pack_roots(me, owner, left_root, right_root, n):
    band, breadth = left_root.shape
    tiles = breadth // TILE
    quarter = tiles // 4
    more = slots_of(n, band, tiles) * TILE * PAIR // breadth

    def kernel(me_ref, owner_ref, l_ref, r_ref, out_ref):
        number = band_of(owner_ref, me_ref[0], n)
        low = lower_half(TILE)
        out_ref[band:] = jnp.zeros((more, breadth), BF16)
        slot = jnp.int32(0)
        for row in range(0, band, TILE):
            tile = (number * (band // TILE) + row // TILE) & (tiles - 1)
            odd, pair = tile & 1, tile >> 1
            rows = slice(row, row + TILE)
            last = lanes(pair + quarter, breadth)
            for at, ref in ((0, l_ref), (quarter, r_ref)):
                start = ref[rows, lanes(pair, breadth)].astype(F32)
                end = ref[rows, last].astype(F32)
                mixed = jnp.where(low & (odd == 1), end, start).astype(BF16)
                out_ref[rows, at * PAIR : (at + 1) * PAIR] = mixed
                for i in range(1, quarter):
                    out_ref[rows, (at + i) * PAIR : (at + i + 1) * PAIR] = ref[rows, lanes(pair + i, breadth)]
            here = meets(tile, tiles)

            @pl.when(here)
            def _():
                left, right = l_ref[rows, last].astype(F32), r_ref[rows, last].astype(F32)
                left = jnp.where(odd == 1, swapped(left), left)
                right = jnp.where(odd == 1, right, swapped(right))
                both = jnp.where(low, left, right).astype(BF16)
                for i in range(TILE // more):
                    place = lanes(slot * (TILE // more) + i, breadth)
                    out_ref[band : band + more, place] = both[i * more : (i + 1) * more]

            slot = slot + here.astype(jnp.int32)

    return pl.pallas_call(
        kernel,
        out_shape=jax.ShapeDtypeStruct((band + more, breadth), BF16),
        grid_spec=pltpu.PrefetchScalarGridSpec(
            num_scalar_prefetch=1,
            grid=(1,),
            in_specs=[whole(1, n), whole(band, breadth), whole(band, breadth)],
            out_specs=whole(band + more, breadth),
        ),
        compiler_params=params(),
        name="pack_roots",
    )(me, owner, left_root, right_root)


def place_packed(pieces, refs, numbers, half_l, half_r, band, breadth):
    tiles = breadth // TILE
    quarter = tiles // 4
    low = lower_half(TILE)
    for offset, number in numbers.items():
        parts = [(first, ref) for (place, first, _), ref in zip(pieces, refs) if place == offset]
        more = max(first + ref.shape[0] for first, ref in parts) - band

        def rows_at(row, end, pairs):
            found = []
            for first, ref in parts:
                top, bottom = max(row, first), min(end, first + ref.shape[0])
                if top < bottom:
                    found.append(ref[top - first : bottom - first, pairs].astype(F32))
            return jnp.concatenate(found, 0) if len(found) > 1 else found[0]

        slot = jnp.int32(0)
        for row in range(0, band, TILE):
            tile = (number * (band // TILE) + row // TILE) & (tiles - 1)
            odd, pair = tile & 1, tile >> 1
            at = pl.ds(pl.multiple_of(number * band + row, TILE), TILE)
            here = meets(tile, tiles)
            both = jnp.concatenate(
                [
                    rows_at(band, band + more, lanes(slot * (TILE // more) + i, breadth))
                    for i in range(TILE // more)
                ],
                0,
            )
            slot = slot + here.astype(jnp.int32)
            other = swapped(both)
            late = low & (odd == 1)
            mine = (low == (odd == 0)) & here
            for start, half, value in (
                (0, half_l, jnp.where(odd == 1, other, both)),
                (quarter, half_r, jnp.where(odd == 1, both, other)),
            ):
                mixed = rows_at(row, row + TILE, slice(start * PAIR, (start + 1) * PAIR))
                half[at, lanes(pair, breadth)] = jnp.where(late, 0.0, mixed).astype(BF16)
                end = jnp.where(mine, value, jnp.where(late, mixed, 0.0))
                half[at, lanes(pair + quarter, breadth)] = end.astype(BF16)
                for i in range(1, quarter):
                    some = rows_at(row, row + TILE, slice((start + i) * PAIR, (start + i + 1) * PAIR))
                    half[at, lanes(pair + i, breadth)] = some.astype(BF16)


def add_send(me, partial, arrived, distance, n, first, *after):
    band, breadth = partial.shape[1] // n, partial.shape[2]
    rows = arrived.shape[0]

    def kernel(me_ref, own_ref, a_ref, *refs):
        out_ref = refs[-1]
        if rows == band:
            out_ref[...] = (own_ref[0].astype(F32) + a_ref[...].astype(F32)).astype(BF16)
        else:
            got, other = slice(first, first + rows), slice(rows - first, band - first)
            out_ref[got] = (own_ref[0, got].astype(F32) + a_ref[...].astype(F32)).astype(BF16)
            out_ref[other] = own_ref[0, other]

    return pl.pallas_call(
        kernel,
        out_shape=jax.ShapeDtypeStruct((band, breadth), BF16),
        grid_spec=pltpu.PrefetchScalarGridSpec(
            num_scalar_prefetch=1,
            grid=(1,),
            in_specs=[
                pl.BlockSpec((1, band, breadth), lambda i, m: (0, away(m[0], distance, n), 0)),
                whole(rows, breadth),
            ]
            + [pl.BlockSpec(memory_space=pl.ANY)] * len(after),
            out_specs=whole(band, breadth),
        ),
        compiler_params=params(),
        name="add_send",
    )(me, partial, arrived, *after)


def add_own(me, partial, right, left, n, *after):
    band, breadth = partial.shape[1] // n, partial.shape[2]

    def kernel(me_ref, own_ref, r_ref, l_ref, *refs):
        out_ref = refs[-1]
        total = own_ref[0].astype(F32) + r_ref[...].astype(F32) + l_ref[...].astype(F32)
        out_ref[...] = total.astype(BF16)

    return pl.pallas_call(
        kernel,
        out_shape=jax.ShapeDtypeStruct((band, breadth), BF16),
        grid_spec=pltpu.PrefetchScalarGridSpec(
            num_scalar_prefetch=1,
            grid=(1,),
            in_specs=[
                pl.BlockSpec((1, band, breadth), lambda i, m: (0, m[0], 0)),
                whole(band, breadth),
                whole(band, breadth),
            ]
            + [pl.BlockSpec(memory_space=pl.ANY)] * len(after),
            out_specs=whole(band, breadth),
        ),
        compiler_params=params(),
        name="add_own",
    )(me, partial, right, left, *after)


def unpack_roots(me, owner, pieces, stacked, breadth, n):
    band = stacked // n
    tiles = breadth // TILE
    nblocks = stacked // breadth

    def kernel(me_ref, owner_ref, *refs):
        refs, (left_ref, right_ref, half_l, half_r) = refs[: len(pieces)], refs[len(pieces) :]
        upper = lax.broadcasted_iota(jnp.int32, (PAIR, PAIR), 0) < TILE
        aside = upper & (lax.broadcasted_iota(jnp.int32, (PAIR, PAIR), 1) >= TILE)
        numbers = {}
        for offset in sorted({p[0] for p in pieces}):
            numbers[offset] = band_of(owner_ref, away(me_ref[0], offset, n), n)
        place_packed(pieces, refs, numbers, half_l, half_r, band, breadth)
        pairs = tiles // 2
        for half, out in ((half_r, right_ref), (half_l, left_ref)):
            for b in range(nblocks):

                def square(i, j):
                    top = b * breadth + i * PAIR
                    return slice(top, top + PAIR), slice(j * PAIR, (j + 1) * PAIR)

                for i in range(pairs):
                    for j in range(pairs):
                        apart = (i - j) % pairs
                        if apart == 0:
                            here = half[square(i, i)]
                            value = here + jnp.where(aside, here, jnp.zeros_like(here)).T
                        elif apart < pairs // 2:
                            value = half[square(j, i)].T
                        elif apart == pairs // 2:
                            value = half[square(i, j)] + half[square(j, i)].T
                        else:
                            value = half[square(i, j)]
                        out[square(i, j)] = value

    out = jax.ShapeDtypeStruct((stacked, breadth), BF16)
    return pl.pallas_call(
        kernel,
        out_shape=(out, out),
        grid_spec=pltpu.PrefetchScalarGridSpec(
            num_scalar_prefetch=1,
            grid=(1,),
            in_specs=[whole(1, n)] + [whole(*x.shape) for _, _, x in pieces],
            out_specs=(whole(stacked, breadth), whole(stacked, breadth)),
            scratch_shapes=[pltpu.VMEM((stacked, breadth), BF16)] * 2,
        ),
        compiler_params=params(),
        name="unpack_roots",
    )(me, owner, *[x for _, _, x in pieces])


def begin(me, pieces, left_root, right_root, n):
    stacked, breadth = left_root.shape
    band = stacked // n
    nblocks = stacked // breadth

    def kernel(me_ref, *refs):
        parts, refs = refs[: len(pieces)], refs[len(pieces) :]
        lroot, rroot, dir_ref, last_ref, grad, rest_ref, done, sems = refs
        for (offset, first, _), ref in zip(pieces, parts):
            place = away(me_ref[0], offset, n) * band + first
            grad[pl.ds(pl.multiple_of(place, CHUNK), ref.shape[0]), :] = ref[...]
        start = away(me_ref[0], n // 2, n) * band
        grad[pl.ds(pl.multiple_of(start, CHUNK), band), :] = jnp.zeros((band, breadth), BF16)
        copies = []
        for b in range(nblocks):
            rows = slice(b * breadth, (b + 1) * breadth)
            mixed = jnp.dot(grad[rows], rroot[rows], preferred_element_type=F32).astype(BF16)
            block = jnp.dot(lroot[rows], mixed, preferred_element_type=F32)
            if b == nblocks - 1:
                last_ref[...] = block.astype(BF16)
            else:
                done[rows] = block.astype(BF16)
                copies.append(pltpu.make_async_copy(done.at[rows], dir_ref.at[rows], sems.at[b]))
                copies[-1].start()
            rest_ref[b] = block
        for copy in copies:
            copy.wait()

    return pl.pallas_call(
        kernel,
        out_shape=(
            jax.ShapeDtypeStruct((stacked, breadth), BF16),
            jax.ShapeDtypeStruct((breadth, breadth), BF16),
            jax.ShapeDtypeStruct((stacked, breadth), BF16),
            jax.ShapeDtypeStruct((nblocks, breadth, breadth), F32),
        ),
        grid_spec=pltpu.PrefetchScalarGridSpec(
            num_scalar_prefetch=1,
            grid=(1,),
            in_specs=[whole(*x.shape) for _, _, x in pieces] + [whole(stacked, breadth)] * 2,
            out_specs=(
                pl.BlockSpec(memory_space=pl.ANY),
                whole(breadth, breadth),
                whole(stacked, breadth),
                whole(nblocks, breadth, breadth),
            ),
            scratch_shapes=[
                pltpu.VMEM((stacked, breadth), BF16),
                pltpu.SemaphoreType.DMA((nblocks,)),
            ],
        ),
        compiler_params=params(),
        name="begin",
    )(me, *[x for _, _, x in pieces], left_root, right_root)


def finish(me, owner, pieces, directions, last, grad, rest, left_root, right_root, left_factor, right_factor, n):
    stacked, breadth = left_root.shape
    band = stacked // n
    nblocks = stacked // breadth

    def kernel(me_ref, owner_ref, *refs):
        parts, refs = refs[: len(pieces)], refs[len(pieces) :]
        _, final_ref, grad_ref, rest_ref, lroot, rroot, lfac, rfac, *refs = refs
        dir_ref, lout_ref, rout_ref, late, block, lout, rout, sems = refs
        far = away(me_ref[0], n // 2, n) * band
        for (_, first, _), ref in zip(pieces, parts):
            late[first : first + ref.shape[0]] = ref[...]
        shift = breadth.bit_length() - 1
        row = (far + lax.broadcasted_iota(jnp.int32, (band, breadth), 0)) >> shift
        there = pl.ds(pl.multiple_of(far, CHUNK), band)
        first_block = far >> shift
        last_block = (far + band - 1) >> shift

        def span(number):
            return pl.ds(pl.multiple_of(number * breadth, breadth), breadth)

        def copy(slot, number):
            return pltpu.make_async_copy(block.at[slot], dir_ref.at[span(number)], sems.at[slot])

        bottom = pl.ds((nblocks - 1) * breadth, breadth)
        keep = pltpu.make_async_copy(final_ref, dir_ref.at[bottom], sems.at[4])

        @pl.when(last_block != nblocks - 1)
        def _():
            keep.start()

        def complete(slot, number):
            some = jnp.where(row == number, late[...].astype(F32), 0.0).astype(BF16)
            mixed = jnp.dot(some, rroot[span(number), :], preferred_element_type=F32).astype(BF16)
            more = lax.dot_general(lroot[there, :], mixed, TN, preferred_element_type=F32)
            block[slot] = (rest_ref[number] + more).astype(BF16)

        start = band_of(owner_ref, me_ref[0], n) * band
        grad_ref[there, :] = late[...]
        mine = grad_ref[pl.ds(pl.multiple_of(start, CHUNK), band), :]
        own_first = start >> shift
        own_last = (start + band - 1) >> shift
        own_row = start + lax.broadcasted_iota(jnp.int32, (band, breadth), 0)
        column = lax.broadcasted_iota(jnp.int32, (band, breadth), 1)

        def renewed(number):
            g = grad_ref[span(number), :]
            left = lax.dot_general(mine, g, NT, preferred_element_type=F32)
            pick = (own_row - number * breadth == column).astype(BF16)
            turned = lax.dot_general(pick, g, NT, preferred_element_type=F32).astype(BF16)
            right = jnp.dot(turned, g, preferred_element_type=F32)
            return BETA * lfac[...] + (1.0 - BETA) * left, BETA * rfac[...] + (1.0 - BETA) * right

        complete(0, first_block)
        lout[...], rout[...] = renewed(own_first)
        copy(0, first_block).start()

        @pl.when(last_block != first_block)
        def _():
            complete(1, last_block)
            copy(1, last_block).start()

        @pl.when(own_last != own_first)
        def _():
            later = own_row >= own_last * breadth
            left, right = renewed(own_last)
            lout[...] = jnp.where(later, left, lout[...])
            rout[...] = jnp.where(later, right, rout[...])

        outs = []
        for slot, (out, ref) in enumerate(((lout, lout_ref), (rout, rout_ref))):
            outs.append(pltpu.make_async_copy(out, ref, sems.at[2 + slot]))
            outs[-1].start()
        copy(0, first_block).wait()

        @pl.when(last_block != first_block)
        def _():
            copy(1, last_block).wait()

        @pl.when(last_block != nblocks - 1)
        def _():
            keep.wait()

        for out in outs:
            out.wait()

    own = jax.ShapeDtypeStruct((band, breadth), F32)
    return pl.pallas_call(
        kernel,
        out_shape=(jax.ShapeDtypeStruct((stacked, breadth), BF16), own, own),
        grid_spec=pltpu.PrefetchScalarGridSpec(
            num_scalar_prefetch=1,
            grid=(1,),
            in_specs=[whole(1, n)]
            + [whole(*x.shape) for _, _, x in pieces]
            + [pl.BlockSpec(memory_space=pl.ANY), whole(breadth, breadth), whole(stacked, breadth)]
            + [whole(nblocks, breadth, breadth)]
            + [whole(stacked, breadth)] * 2
            + [whole(band, breadth)] * 2,
            out_specs=[pl.BlockSpec(memory_space=pl.ANY)] * 3,
            scratch_shapes=[
                pltpu.VMEM((band, breadth), BF16),
                pltpu.VMEM((2, breadth, breadth), BF16),
                pltpu.VMEM((band, breadth), F32),
                pltpu.VMEM((band, breadth), F32),
                pltpu.SemaphoreType.DMA((5,)),
            ],
        ),
        input_output_aliases={2 + len(pieces): 0},
        compiler_params=params(),
        name="finish",
    )(
        me,
        owner,
        *[x for _, _, x in pieces],
        directions,
        last,
        grad,
        rest,
        left_root,
        right_root,
        left_factor,
        right_factor,
    )


def ring(n, partial_grads, band_owner, left_factor, right_factor, left_root, right_root):
    stacked, breadth = partial_grads.shape[1:]
    band = stacked // n
    half = band // 2
    me = lax.axis_index("dp").astype(jnp.int32).reshape(1)
    owner = band_owner.reshape(1, n)
    order = [2 * q for q in range(n // 2)] + [2 * (n - 1 - q) + 1 for q in range(n // 2, n)]
    onward = [(order[q], order[(q + 1) % n]) for q in range(n)]
    backward = [(b, a) for a, b in onward]

    def send_right(x):
        return lax.ppermute(x, "dp", onward)

    def send_left(x):
        return lax.ppermute(x, "dp", backward)

    def gather(own, parts):
        rows = own.shape[0] // 2
        pieces = [(0, 0, own)]
        if parts == 1:
            right, left = own, own
            for hop in range(1, n // 2):
                right, left = send_right(right), send_left(left)
                pieces += [(-hop, 0, right), (hop, 0, left)]
            right, left = send_right(right[:rows]), send_left(left[rows:])
        else:
            upper, lower = own[:rows], own[rows:]
            ways = [upper, upper, lower, lower]
            for hop in range(1, n // 2):
                ways = [
                    send_left(ways[3]),
                    send_right(ways[2]),
                    send_left(ways[1]),
                    send_right(ways[0]),
                ][::-1]
                pieces += [(-hop, 0, ways[0]), (hop, 0, ways[1])]
                pieces += [(-hop, rows, ways[2]), (hop, rows, ways[3])]
            right, left = send_right(ways[0]), send_left(ways[3])
        return pieces + [(n // 2, 0, right), (n // 2, rows, left)]

    right, left = first_sends(me, partial_grads, n)
    packed = pack_roots(me, owner, left_root, right_root, n)
    right, left = send_right(right), send_left(left)
    root_pieces = gather(packed, 1)
    for distance in range(n // 2 - 1, 0, -1):
        right = add_send(me, partial_grads, right, distance, n, 0)
        left = add_send(me, partial_grads, left, -distance, n, half if left.shape[0] == half else 0)
        right, left = send_right(right), send_left(left)
    roots = unpack_roots(me, owner, root_pieces, stacked, breadth, n)
    own = add_own(me, partial_grads, right, left, n)
    pieces = gather(own, GRAD_PARTS)
    begun = begin(me, pieces[:-2], *roots, n)
    return finish(me, owner, pieces[-2:], *begun, *roots, left_factor, right_factor, n)


def shards(n, partial_grads, *rest):
    stacked, breadth = partial_grads.shape[1:]
    band = stacked // n
    fits = band % TILE == 0 and breadth % (4 * TILE) == 0 and breadth & (breadth - 1) == 0
    if fits:
        more = slots_of(n, band, breadth // TILE) * TILE * PAIR // breadth
        fits = more > 0 and TILE % more == 0 and (band + more) % 32 == 0
    if 4 <= n <= 16 and n % 2 == 0 and fits:
        return ring(n, partial_grads, *rest)
    return general(partial_grads, *rest)


def solution(mesh):
    placed = (P("dp", None, "mp"), P(), P("dp", "mp"), P("dp", "mp"), P("dp", "mp"), P("dp", "mp"))
    return jax.shard_map(
        functools.partial(shards, mesh.shape["dp"]),
        mesh=mesh,
        in_specs=placed,
        out_specs=(P(None, "mp"), P("dp", "mp"), P("dp", "mp")),
        check_vma=False,
    )
```

```python
import functools

import jax
import jax.numpy as jnp
from jax import lax
from jax.experimental import pallas as pl
from jax.experimental.pallas import tpu as pltpu
from jax.sharding import PartitionSpec as P

BETA = 0.95
TILE = 64
CHUNK = 32
GRAD_PARTS = 2
F32 = jnp.float32
BF16 = jnp.bfloat16
NT = (((1,), (1,)), ((), ()))
TN = (((0,), (0,)), ((), ()))
VMEM_LIMIT = 40 * 1024 * 1024


def against(band_rows, whole_rows, select):
    nblocks = select.shape[1]
    breadth = whole_rows.shape[1]
    blocks = whole_rows.reshape(nblocks, breadth, breadth)
    products = jnp.einsum("rk,bck->rbc", band_rows, blocks, preferred_element_type=jnp.float32)
    return jnp.sum(select[:, :, None] * products, axis=1)


def to_band_order(gathered, owners, members):
    shaped = gathered.reshape(members, -1, gathered.shape[1])
    return jnp.take(shaped, owners, axis=0).reshape(gathered.shape)


def general(partial_grads, band_owner, left_factor, right_factor, left_root, right_root):
    members = lax.axis_size("dp")
    band_size = left_factor.shape[0]
    breadth = left_factor.shape[1]
    stacked = partial_grads.shape[1]
    nblocks = stacked // breadth
    devices = jnp.arange(members, dtype=jnp.int32)
    inverse = jnp.sum(
        jnp.where(band_owner[None, :] == devices[:, None], devices[None, :], 0), axis=1
    )
    own_band = inverse[lax.axis_index("dp")]
    partial_value = partial_grads[0]
    even_rows = lax.psum_scatter(
        partial_value.astype(jnp.float32), "dp", scatter_dimension=0, tiled=True
    ).astype(jnp.bfloat16)
    grad_full = lax.all_gather(even_rows, "dp", axis=0, tiled=True)
    grad_rows = lax.dynamic_slice_in_dim(grad_full, own_band * band_size, band_size, 0)
    global_rows = own_band * band_size + jnp.arange(band_size, dtype=jnp.int32)
    block_ids = global_rows // breadth
    within = global_rows % breadth
    block_range = jnp.arange(nblocks, dtype=jnp.int32)
    select = (block_ids[:, None] == block_range[None, :]).astype(jnp.float32)
    left_term = against(grad_rows, grad_full, select)
    left_updated = BETA * left_factor + (1.0 - BETA) * left_term
    column_range = jnp.arange(breadth, dtype=jnp.int32)
    onehot = (
        (block_range[:, None, None] == block_ids[None, None, :])
        & (column_range[None, :, None] == within[None, None, :])
    ).astype(jnp.bfloat16)
    blocks = grad_full.reshape(nblocks, breadth, breadth)
    columns = jnp.einsum("bkc,bcr->kr", blocks, onehot, preferred_element_type=jnp.float32).astype(
        jnp.bfloat16
    )
    right_products = jnp.einsum("kr,bkc->rbc", columns, blocks, preferred_element_type=jnp.float32)
    right_term = jnp.sum(select[:, :, None] * right_products, axis=1)
    right_updated = BETA * right_factor + (1.0 - BETA) * right_term
    mixed_rows = against(right_root, grad_full, select).astype(jnp.bfloat16)
    mixed_full = to_band_order(
        lax.all_gather(mixed_rows, "dp", axis=0, tiled=True), band_owner, members
    )
    direction_rows = against(left_root, mixed_full, select).astype(jnp.bfloat16)
    direction = to_band_order(
        lax.all_gather(direction_rows, "dp", axis=0, tiled=True), band_owner, members
    )
    return (direction, left_updated, right_updated)


def seat_of(device, n):
    return jnp.where((device & 1) == 0, device >> 1, n - ((device + 1) >> 1))


def device_at(seat, n):
    seat = jnp.where(seat < 0, seat + n, seat)
    seat = jnp.where(seat >= n, seat - n, seat)
    return jnp.where(seat < n // 2, 2 * seat, 2 * (n - 1 - seat) + 1)


def away(me, offset, n):
    return device_at(seat_of(me, n) + offset, n)


def band_of(owner_ref, device, n):
    order = lax.broadcasted_iota(jnp.int32, (1, n), 1)
    hit = owner_ref[...] == device
    return jnp.sum(jnp.where(hit, order, 0).astype(F32)).astype(jnp.int32)


def whole(*shape):
    return pl.BlockSpec(shape, lambda i, *_: (0,) * len(shape))


def params(limit=VMEM_LIMIT):
    return pltpu.CompilerParams(vmem_limit_bytes=limit)


PAIR = 2 * TILE


def meets(tile, tiles):
    half, quarter = tiles // 2, tiles // 4
    return ((tile < half) & (tile != quarter)) | (tile == half + quarter)


def slots_of(n, band, tiles):
    rows = band // TILE
    return max(sum(meets((k * rows + t) % tiles, tiles) for t in range(rows)) for k in range(n))


def lanes(pair, breadth):
    return pl.ds(pl.multiple_of((pair & (breadth // PAIR - 1)) * PAIR, PAIR), PAIR)


def lower_half(rows):
    return lax.broadcasted_iota(jnp.int32, (rows, PAIR), 1) < TILE


def swapped(x):
    return pltpu.roll(x, TILE, 1)


def first_sends(me, partial, n):
    breadth = partial.shape[2]
    band = partial.shape[1] // n
    half = band // 2

    def kernel(me_ref, far_ref, right_ref, left_ref):
        right_ref[...] = far_ref[0, :half]
        left_ref[...] = far_ref[0, half:]

    sent = jax.ShapeDtypeStruct((half, breadth), BF16)
    return pl.pallas_call(
        kernel,
        out_shape=(sent, sent),
        grid_spec=pltpu.PrefetchScalarGridSpec(
            num_scalar_prefetch=1,
            grid=(1,),
            in_specs=[
                pl.BlockSpec((1, band, breadth), lambda i, m: (0, away(m[0], n // 2, n), 0)),
            ],
            out_specs=(whole(half, breadth), whole(half, breadth)),
        ),
        compiler_params=params(),
        name="first_sends",
    )(me, partial)


def pack_roots(me, owner, left_root, right_root, n):
    band, breadth = left_root.shape
    tiles = breadth // TILE
    quarter = tiles // 4
    more = slots_of(n, band, tiles) * TILE * PAIR // breadth

    def kernel(me_ref, owner_ref, l_ref, r_ref, out_ref):
        number = band_of(owner_ref, me_ref[0], n)
        low = lower_half(TILE)
        out_ref[band:] = jnp.zeros((more, breadth), BF16)
        slot = jnp.int32(0)
        for row in range(0, band, TILE):
            tile = (number * (band // TILE) + row // TILE) & (tiles - 1)
            odd, pair = tile & 1, tile >> 1
            rows = slice(row, row + TILE)
            last = lanes(pair + quarter, breadth)
            for at, ref in ((0, l_ref), (quarter, r_ref)):
                start = ref[rows, lanes(pair, breadth)].astype(F32)
                end = ref[rows, last].astype(F32)
                mixed = jnp.where(low & (odd == 1), end, start).astype(BF16)
                out_ref[rows, at * PAIR : (at + 1) * PAIR] = mixed
                for i in range(1, quarter):
                    out_ref[rows, (at + i) * PAIR : (at + i + 1) * PAIR] = ref[rows, lanes(pair + i, breadth)]
            here = meets(tile, tiles)

            @pl.when(here)
            def _():
                left, right = l_ref[rows, last].astype(F32), r_ref[rows, last].astype(F32)
                left = jnp.where(odd == 1, swapped(left), left)
                right = jnp.where(odd == 1, right, swapped(right))
                both = jnp.where(low, left, right).astype(BF16)
                for i in range(TILE // more):
                    place = lanes(slot * (TILE // more) + i, breadth)
                    out_ref[band : band + more, place] = both[i * more : (i + 1) * more]

            slot = slot + here.astype(jnp.int32)

    return pl.pallas_call(
        kernel,
        out_shape=jax.ShapeDtypeStruct((band + more, breadth), BF16),
        grid_spec=pltpu.PrefetchScalarGridSpec(
            num_scalar_prefetch=1,
            grid=(1,),
            in_specs=[whole(1, n), whole(band, breadth), whole(band, breadth)],
            out_specs=whole(band + more, breadth),
        ),
        compiler_params=params(),
        name="pack_roots",
    )(me, owner, left_root, right_root)


def place_packed(pieces, refs, numbers, half_l, half_r, band, breadth):
    tiles = breadth // TILE
    quarter = tiles // 4
    low = lower_half(TILE)
    for offset, number in numbers.items():
        parts = [(first, ref) for (place, first, _), ref in zip(pieces, refs) if place == offset]
        more = max(first + ref.shape[0] for first, ref in parts) - band

        def rows_at(row, end, pairs):
            found = []
            for first, ref in parts:
                top, bottom = max(row, first), min(end, first + ref.shape[0])
                if top < bottom:
                    found.append(ref[top - first : bottom - first, pairs].astype(F32))
            return jnp.concatenate(found, 0) if len(found) > 1 else found[0]

        slot = jnp.int32(0)
        for row in range(0, band, TILE):
            tile = (number * (band // TILE) + row // TILE) & (tiles - 1)
            odd, pair = tile & 1, tile >> 1
            at = pl.ds(pl.multiple_of(number * band + row, TILE), TILE)
            here = meets(tile, tiles)
            both = jnp.concatenate(
                [
                    rows_at(band, band + more, lanes(slot * (TILE // more) + i, breadth))
                    for i in range(TILE // more)
                ],
                0,
            )
            slot = slot + here.astype(jnp.int32)
            other = swapped(both)
            late = low & (odd == 1)
            mine = (low == (odd == 0)) & here
            for start, half, value in (
                (0, half_l, jnp.where(odd == 1, other, both)),
                (quarter, half_r, jnp.where(odd == 1, both, other)),
            ):
                mixed = rows_at(row, row + TILE, slice(start * PAIR, (start + 1) * PAIR))
                half[at, lanes(pair, breadth)] = jnp.where(late, 0.0, mixed).astype(BF16)
                end = jnp.where(mine, value, jnp.where(late, mixed, 0.0))
                half[at, lanes(pair + quarter, breadth)] = end.astype(BF16)
                for i in range(1, quarter):
                    some = rows_at(row, row + TILE, slice((start + i) * PAIR, (start + i + 1) * PAIR))
                    half[at, lanes(pair + i, breadth)] = some.astype(BF16)


def add_send(me, partial, arrived, distance, n, first, *after):
    band, breadth = partial.shape[1] // n, partial.shape[2]
    rows = arrived.shape[0]

    def kernel(me_ref, own_ref, a_ref, *refs):
        out_ref = refs[-1]
        if rows == band:
            out_ref[...] = (own_ref[0].astype(F32) + a_ref[...].astype(F32)).astype(BF16)
        else:
            got, other = slice(first, first + rows), slice(rows - first, band - first)
            out_ref[got] = (own_ref[0, got].astype(F32) + a_ref[...].astype(F32)).astype(BF16)
            out_ref[other] = own_ref[0, other]

    return pl.pallas_call(
        kernel,
        out_shape=jax.ShapeDtypeStruct((band, breadth), BF16),
        grid_spec=pltpu.PrefetchScalarGridSpec(
            num_scalar_prefetch=1,
            grid=(1,),
            in_specs=[
                pl.BlockSpec((1, band, breadth), lambda i, m: (0, away(m[0], distance, n), 0)),
                whole(rows, breadth),
            ]
            + [pl.BlockSpec(memory_space=pl.ANY)] * len(after),
            out_specs=whole(band, breadth),
        ),
        compiler_params=params(),
        name="add_send",
    )(me, partial, arrived, *after)


def add_own(me, partial, right, left, n, *after):
    band, breadth = partial.shape[1] // n, partial.shape[2]

    def kernel(me_ref, own_ref, r_ref, l_ref, *refs):
        out_ref = refs[-1]
        total = own_ref[0].astype(F32) + r_ref[...].astype(F32) + l_ref[...].astype(F32)
        out_ref[...] = total.astype(BF16)

    return pl.pallas_call(
        kernel,
        out_shape=jax.ShapeDtypeStruct((band, breadth), BF16),
        grid_spec=pltpu.PrefetchScalarGridSpec(
            num_scalar_prefetch=1,
            grid=(1,),
            in_specs=[
                pl.BlockSpec((1, band, breadth), lambda i, m: (0, m[0], 0)),
                whole(band, breadth),
                whole(band, breadth),
            ]
            + [pl.BlockSpec(memory_space=pl.ANY)] * len(after),
            out_specs=whole(band, breadth),
        ),
        compiler_params=params(),
        name="add_own",
    )(me, partial, right, left, *after)


def unpack_roots(me, owner, pieces, stacked, breadth, n):
    band = stacked // n
    tiles = breadth // TILE
    nblocks = stacked // breadth

    def kernel(me_ref, owner_ref, *refs):
        refs, (left_ref, right_ref, half_l, half_r) = refs[: len(pieces)], refs[len(pieces) :]
        upper = lax.broadcasted_iota(jnp.int32, (PAIR, PAIR), 0) < TILE
        aside = upper & (lax.broadcasted_iota(jnp.int32, (PAIR, PAIR), 1) >= TILE)
        numbers = {}
        for offset in sorted({p[0] for p in pieces}):
            numbers[offset] = band_of(owner_ref, away(me_ref[0], offset, n), n)
        place_packed(pieces, refs, numbers, half_l, half_r, band, breadth)
        pairs = tiles // 2
        for half, out in ((half_r, right_ref), (half_l, left_ref)):
            for b in range(nblocks):

                def square(i, j):
                    top = b * breadth + i * PAIR
                    return slice(top, top + PAIR), slice(j * PAIR, (j + 1) * PAIR)

                for i in range(pairs):
                    for j in range(pairs):
                        apart = (i - j) % pairs
                        if apart == 0:
                            here = half[square(i, i)]
                            value = here + jnp.where(aside, here, jnp.zeros_like(here)).T
                        elif apart < pairs // 2:
                            value = half[square(j, i)].T
                        elif apart == pairs // 2:
                            value = half[square(i, j)] + half[square(j, i)].T
                        else:
                            value = half[square(i, j)]
                        out[square(i, j)] = value

    out = jax.ShapeDtypeStruct((stacked, breadth), BF16)
    return pl.pallas_call(
        kernel,
        out_shape=(out, out),
        grid_spec=pltpu.PrefetchScalarGridSpec(
            num_scalar_prefetch=1,
            grid=(1,),
            in_specs=[whole(1, n)] + [whole(*x.shape) for _, _, x in pieces],
            out_specs=(whole(stacked, breadth), whole(stacked, breadth)),
            scratch_shapes=[pltpu.VMEM((stacked, breadth), BF16)] * 2,
        ),
        compiler_params=params(),
        name="unpack_roots",
    )(me, owner, *[x for _, _, x in pieces])


def begin(me, pieces, left_root, right_root, n):
    stacked, breadth = left_root.shape
    band = stacked // n
    nblocks = stacked // breadth

    def kernel(me_ref, *refs):
        parts, refs = refs[: len(pieces)], refs[len(pieces) :]
        lroot, rroot, dir_ref, last_ref, grad, rest_ref, done, sems = refs
        for (offset, first, _), ref in zip(pieces, parts):
            place = away(me_ref[0], offset, n) * band + first
            grad[pl.ds(pl.multiple_of(place, CHUNK), ref.shape[0]), :] = ref[...]
        start = away(me_ref[0], n // 2, n) * band
        grad[pl.ds(pl.multiple_of(start, CHUNK), band), :] = jnp.zeros((band, breadth), BF16)
        copies = []
        for b in range(nblocks):
            rows = slice(b * breadth, (b + 1) * breadth)
            mixed = jnp.dot(grad[rows], rroot[rows], preferred_element_type=F32).astype(BF16)
            block = jnp.dot(lroot[rows], mixed, preferred_element_type=F32)
            if b == nblocks - 1:
                last_ref[...] = block.astype(BF16)
            else:
                done[rows] = block.astype(BF16)
                copies.append(pltpu.make_async_copy(done.at[rows], dir_ref.at[rows], sems.at[b]))
                copies[-1].start()
            rest_ref[b] = block
        for copy in copies:
            copy.wait()

    return pl.pallas_call(
        kernel,
        out_shape=(
            jax.ShapeDtypeStruct((stacked, breadth), BF16),
            jax.ShapeDtypeStruct((breadth, breadth), BF16),
            jax.ShapeDtypeStruct((stacked, breadth), BF16),
            jax.ShapeDtypeStruct((nblocks, breadth, breadth), F32),
        ),
        grid_spec=pltpu.PrefetchScalarGridSpec(
            num_scalar_prefetch=1,
            grid=(1,),
            in_specs=[whole(*x.shape) for _, _, x in pieces] + [whole(stacked, breadth)] * 2,
            out_specs=(
                pl.BlockSpec(memory_space=pl.ANY),
                whole(breadth, breadth),
                whole(stacked, breadth),
                whole(nblocks, breadth, breadth),
            ),
            scratch_shapes=[
                pltpu.VMEM((stacked, breadth), BF16),
                pltpu.SemaphoreType.DMA((nblocks,)),
            ],
        ),
        compiler_params=params(),
        name="begin",
    )(me, *[x for _, _, x in pieces], left_root, right_root)


def finish(me, owner, pieces, directions, last, grad, rest, left_root, right_root, left_factor, right_factor, n):
    stacked, breadth = left_root.shape
    band = stacked // n
    nblocks = stacked // breadth

    def kernel(me_ref, owner_ref, *refs):
        parts, refs = refs[: len(pieces)], refs[len(pieces) :]
        _, final_ref, grad_ref, rest_ref, lroot, rroot, lfac, rfac, *refs = refs
        dir_ref, lout_ref, rout_ref, late, block, lout, rout, sems = refs
        far = away(me_ref[0], n // 2, n) * band
        for (_, first, _), ref in zip(pieces, parts):
            late[first : first + ref.shape[0]] = ref[...]
        shift = breadth.bit_length() - 1
        row = (far + lax.broadcasted_iota(jnp.int32, (band, breadth), 0)) >> shift
        there = pl.ds(pl.multiple_of(far, CHUNK), band)
        first_block = far >> shift
        last_block = (far + band - 1) >> shift

        def span(number):
            return pl.ds(pl.multiple_of(number * breadth, breadth), breadth)

        def copy(slot, number):
            return pltpu.make_async_copy(block.at[slot], dir_ref.at[span(number)], sems.at[slot])

        bottom = pl.ds((nblocks - 1) * breadth, breadth)
        keep = pltpu.make_async_copy(final_ref, dir_ref.at[bottom], sems.at[4])

        @pl.when(last_block != nblocks - 1)
        def _():
            keep.start()

        def complete(slot, number):
            some = jnp.where(row == number, late[...].astype(F32), 0.0).astype(BF16)
            mixed = jnp.dot(some, rroot[span(number), :], preferred_element_type=F32).astype(BF16)
            more = lax.dot_general(lroot[there, :], mixed, TN, preferred_element_type=F32)
            block[slot] = (rest_ref[number] + more).astype(BF16)

        start = band_of(owner_ref, me_ref[0], n) * band
        grad_ref[there, :] = late[...]
        mine = grad_ref[pl.ds(pl.multiple_of(start, CHUNK), band), :]
        own_first = start >> shift
        own_last = (start + band - 1) >> shift
        own_row = start + lax.broadcasted_iota(jnp.int32, (band, breadth), 0)
        column = lax.broadcasted_iota(jnp.int32, (band, breadth), 1)

        def renewed(number):
            g = grad_ref[span(number), :]
            left = lax.dot_general(mine, g, NT, preferred_element_type=F32)
            pick = (own_row - number * breadth == column).astype(BF16)
            turned = lax.dot_general(pick, g, NT, preferred_element_type=F32).astype(BF16)
            right = jnp.dot(turned, g, preferred_element_type=F32)
            return BETA * lfac[...] + (1.0 - BETA) * left, BETA * rfac[...] + (1.0 - BETA) * right

        complete(0, first_block)
        copy(0, first_block).start()
        lout[...], rout[...] = renewed(own_first)

        @pl.when(last_block != first_block)
        def _():
            complete(1, last_block)
            copy(1, last_block).start()

        @pl.when(own_last != own_first)
        def _():
            later = own_row >= own_last * breadth
            left, right = renewed(own_last)
            lout[...] = jnp.where(later, left, lout[...])
            rout[...] = jnp.where(later, right, rout[...])

        outs = []
        for slot, (out, ref) in enumerate(((lout, lout_ref), (rout, rout_ref))):
            outs.append(pltpu.make_async_copy(out, ref, sems.at[2 + slot]))
            outs[-1].start()
        copy(0, first_block).wait()

        @pl.when(last_block != first_block)
        def _():
            copy(1, last_block).wait()

        @pl.when(last_block != nblocks - 1)
        def _():
            keep.wait()

        for out in outs:
            out.wait()

    own = jax.ShapeDtypeStruct((band, breadth), F32)
    return pl.pallas_call(
        kernel,
        out_shape=(jax.ShapeDtypeStruct((stacked, breadth), BF16), own, own),
        grid_spec=pltpu.PrefetchScalarGridSpec(
            num_scalar_prefetch=1,
            grid=(1,),
            in_specs=[whole(1, n)]
            + [whole(*x.shape) for _, _, x in pieces]
            + [pl.BlockSpec(memory_space=pl.ANY), whole(breadth, breadth), whole(stacked, breadth)]
            + [whole(nblocks, breadth, breadth)]
            + [whole(stacked, breadth)] * 2
            + [whole(band, breadth)] * 2,
            out_specs=[pl.BlockSpec(memory_space=pl.ANY)] * 3,
            scratch_shapes=[
                pltpu.VMEM((band, breadth), BF16),
                pltpu.VMEM((2, breadth, breadth), BF16),
                pltpu.VMEM((band, breadth), F32),
                pltpu.VMEM((band, breadth), F32),
                pltpu.SemaphoreType.DMA((5,)),
            ],
        ),
        input_output_aliases={2 + len(pieces): 0},
        compiler_params=params(),
        name="finish",
    )(
        me,
        owner,
        *[x for _, _, x in pieces],
        directions,
        last,
        grad,
        rest,
        left_root,
        right_root,
        left_factor,
        right_factor,
    )


def ring(n, partial_grads, band_owner, left_factor, right_factor, left_root, right_root):
    stacked, breadth = partial_grads.shape[1:]
    band = stacked // n
    half = band // 2
    me = lax.axis_index("dp").astype(jnp.int32).reshape(1)
    owner = band_owner.reshape(1, n)
    order = [2 * q for q in range(n // 2)] + [2 * (n - 1 - q) + 1 for q in range(n // 2, n)]
    onward = [(order[q], order[(q + 1) % n]) for q in range(n)]
    backward = [(b, a) for a, b in onward]

    def send_right(x):
        return lax.ppermute(x, "dp", onward)

    def send_left(x):
        return lax.ppermute(x, "dp", backward)

    def gather(own, parts):
        rows = own.shape[0] // 2
        pieces = [(0, 0, own)]
        if parts == 1:
            right, left = own, own
            for hop in range(1, n // 2):
                right, left = send_right(right), send_left(left)
                pieces += [(-hop, 0, right), (hop, 0, left)]
            right, left = send_right(right[:rows]), send_left(left[rows:])
        else:
            upper, lower = own[:rows], own[rows:]
            ways = [upper, upper, lower, lower]
            for hop in range(1, n // 2):
                ways = [
                    send_left(ways[3]),
                    send_right(ways[2]),
                    send_left(ways[1]),
                    send_right(ways[0]),
                ][::-1]
                pieces += [(-hop, 0, ways[0]), (hop, 0, ways[1])]
                pieces += [(-hop, rows, ways[2]), (hop, rows, ways[3])]
            right, left = send_right(ways[0]), send_left(ways[3])
        return pieces + [(n // 2, 0, right), (n // 2, rows, left)]

    right, left = first_sends(me, partial_grads, n)
    packed = pack_roots(me, owner, left_root, right_root, n)
    right, left = send_right(right), send_left(left)
    root_pieces = gather(packed, 1)
    for distance in range(n // 2 - 1, 0, -1):
        right = add_send(me, partial_grads, right, distance, n, 0)
        left = add_send(me, partial_grads, left, -distance, n, half if left.shape[0] == half else 0)
        right, left = send_right(right), send_left(left)
    roots = unpack_roots(me, owner, root_pieces, stacked, breadth, n)
    own = add_own(me, partial_grads, right, left, n)
    pieces = gather(own, GRAD_PARTS)
    begun = begin(me, pieces[:-2], *roots, n)
    return finish(me, owner, pieces[-2:], *begun, *roots, left_factor, right_factor, n)


def shards(n, partial_grads, *rest):
    stacked, breadth = partial_grads.shape[1:]
    band = stacked // n
    fits = band % TILE == 0 and breadth % (4 * TILE) == 0 and breadth & (breadth - 1) == 0
    if fits:
        more = slots_of(n, band, breadth // TILE) * TILE * PAIR // breadth
        fits = more > 0 and TILE % more == 0 and (band + more) % 32 == 0
    if 4 <= n <= 16 and n % 2 == 0 and fits:
        return ring(n, partial_grads, *rest)
    return general(partial_grads, *rest)


def solution(mesh):
    placed = (P("dp", None, "mp"), P(), P("dp", "mp"), P("dp", "mp"), P("dp", "mp"), P("dp", "mp"))
    return jax.shard_map(
        functools.partial(shards, mesh.shape["dp"]),
        mesh=mesh,
        in_specs=placed,
        out_specs=(P(None, "mp"), P("dp", "mp"), P("dp", "mp")),
        check_vma=False,
    )
```
